256 devices in a mesh: row: 8 (over x, y_lo), col: 32 (over z, y_hi, core).
Axes of the slice: x: 4, y: 4 (y_hi: 2, y_lo: 2; y = y_hi * 2 + y_lo), z: 8, core: 2. Of those that a mesh axis runs over, the one named last changes fastest.
Arguments:
- patterns: float32 [16, 64, 256, 256], P('row', 'col'), may hold values from 0.05 to 4
- background: float32 [256, 256], replicated, may hold values from 0.05 to 0.6
- offsets: int32 [16, 64, 2], P('row', 'col'), may hold values from 0 to 64
- probe_wave: float32 [2, 256, 256], replicated, may hold values from -21 to 21
- object_field: float32 [2, 1024, 4096], P(None, 'row', 'col'), may hold values from -15 to 15
Outputs:
- new_object: float32 [2, 1024, 4096], P(None, 'row', 'col')
- new_probe: float32 [2, 256, 256], replicated
The draws below stay inside these ranges and needn't reach their ends.
All inputs are finite; a program needn't handle non-finite values.
Results may differ from the reference program's by a relative error of at most 0.0085.
The reference program's roundings to bfloat16 on the way count: a program that leaves them out, or rounds other values in their place, can miss the bound.
Values sent between devices are 32-bit elements; how exact they have to be, the bound alone decides.
No kernel may reach another device: no remote copies, remote signals or barrier semaphores. Data moves between devices by JAX's collectives and lax.ppermute only.
A program may use at most 64 MiB of HBM per device.

```python
import math
import jax
import jax.numpy as jnp
from jax import lax

K = 256
STEP = 64
ITERS = 2
SR = 16
SC = 64
NR = 1024
NC = 4096


def draw_probe_wave(key, part):
    keys = jax.random.split(jax.random.fold_in(key, 17), 3)
    positions = jnp.arange(K, dtype=jnp.float32) / K
    ramp_up = jnp.exp(jnp.log(3.0) * positions)
    base_draw = jnp.clip(jax.random.normal(keys[0], (2, K, K), jnp.float32), -4.0, 4.0)
    factor_width = 0.8
    row_factor = ramp_up * jnp.exp(factor_width * jax.random.uniform(keys[1], (K,), jnp.float32, -1.0, 1.0))
    col_factor = jnp.exp(factor_width * jax.random.uniform(keys[2], (K,), jnp.float32, -1.0, 1.0))
    return 0.35 * base_draw * row_factor[None, :, None] * col_factor[None, None, :]


def draw_object_field(key, part):
    keys = jax.random.split(jax.random.fold_in(key, 23), 1)
    row_places = jnp.arange(NR, dtype=jnp.float32) / NR
    row_ramp = 0.4 * jnp.exp(jnp.float32(math.log(9.0)) * row_places)
    base_draw = jnp.clip(jax.random.normal(keys[0], (2, NR, NC), jnp.float32), -4.0, 4.0)
    return base_draw * row_ramp[None, :, None]


def plant(drawn, key, least, largest):
    longest = drawn.shape.index(max(drawn.shape))
    spots = []
    for shift in (0, 1):
        where = [jax.random.randint(jax.random.fold_in(key, axis), (), 0, length) for axis, length in enumerate(drawn.shape)]
        where[longest] = (where[longest] + shift) % drawn.shape[longest]
        spots.append(tuple(where))
    return drawn.at[spots[0]].set(least).at[spots[1]].set(largest)


def steps_of(own_key, dims, pieces, least, top_value):
    level, own = 1.0, jax.random.fold_in(own_key, 6)
    for dim, parts in pieces:
        heights = jnp.exp(jax.random.uniform(jax.random.fold_in(own, dim), (parts,), jnp.float32, least / len(pieces), top_value / len(pieces)))
        level = level * jnp.repeat(heights, dims[dim] // parts).reshape([-1 if axis == dim else 1 for axis in range(len(dims))])
    return level


def setup_inputs(seed: int = 0) -> dict:
    arg_keys = jax.random.split(jax.random.key(seed), 6)
    patterns = jnp.clip(jnp.exp(math.log(4.0) - 4.3820266 * jax.random.uniform(arg_keys[0], (SR, SC, K, K), jnp.float32) ** steps_of(arg_keys[0], (SR, SC, K, K), ((0, 8), (1, 32)), -0.2, 0.2)), 0.05, 4.0)
    background = jnp.clip(jax.random.uniform(arg_keys[1], (K, K), jnp.float32, 0.05, 0.6), 0.05, 0.6)
    offsets = plant(jax.random.randint(arg_keys[2], (SR, SC, 2), 0, STEP + 1), jax.random.fold_in(arg_keys[2], 1), 0, STEP).astype(jnp.int32)
    probe_wave = draw_probe_wave(jax.random.fold_in(arg_keys[5], 71), 0)
    object_field = draw_object_field(jax.random.fold_in(arg_keys[5], 71), 0)
    return dict(patterns=patterns, background=background, offsets=offsets, probe_wave=probe_wave, object_field=object_field)


def dft_tables(side_len):
    indices = jnp.arange(side_len, dtype=jnp.int32)
    phases = indices[:, None] * indices[None, :] % side_len
    angles = phases.astype(jnp.float32) * jnp.float32(2.0 * math.pi / side_len)
    scaling = jnp.float32(1.0 / math.sqrt(side_len))
    return ((jnp.cos(angles) * scaling).astype(jnp.bfloat16), (-jnp.sin(angles) * scaling).astype(jnp.bfloat16))

def block_tables(real_part, imag_part):
    left_table = jnp.stack([jnp.stack([real_part, -imag_part]), jnp.stack([imag_part, real_part])])
    right_table = jnp.stack([jnp.stack([real_part, imag_part]), jnp.stack([-imag_part, real_part])])
    return (left_table, right_table)

def product(leading, trailing):
    real_part = leading[..., 0, :, :] * trailing[..., 0, :, :] - leading[..., 1, :, :] * trailing[..., 1, :, :]
    imag_part = leading[..., 0, :, :] * trailing[..., 1, :, :] + leading[..., 1, :, :] * trailing[..., 0, :, :]
    return jnp.stack([real_part, imag_part], axis=-3)

def times_conj(leading, trailing):
    real_part = leading[..., 0, :, :] * trailing[..., 0, :, :] + leading[..., 1, :, :] * trailing[..., 1, :, :]
    imag_part = leading[..., 0, :, :] * trailing[..., 1, :, :] - leading[..., 1, :, :] * trailing[..., 0, :, :]
    return jnp.stack([real_part, imag_part], axis=-3)

def transform(wave_set, left_table, right_table):
    half_way = jnp.einsum('cdkj,djn->ckn', left_table.astype(jnp.float32), wave_set.astype(jnp.float32), precision=lax.Precision.HIGHEST).astype(jnp.bfloat16)
    return jnp.einsum('ckn,cdnm->dkm', half_way.astype(jnp.float32), right_table.astype(jnp.float32), precision=lax.Precision.HIGHEST)

def reference(patterns, background, offsets, probe_wave, object_field):
    margin = K // 2
    real_part, imag_part = dft_tables(K)
    forward = block_tables(real_part, imag_part)
    inverse = block_tables(real_part, -imag_part)
    start_rows = (jnp.arange(SR, dtype=jnp.int32)[:, None] * STEP + offsets[:, :, 0].astype(jnp.int32)).reshape(SR * SC).astype(jnp.int32)
    start_cols = (jnp.arange(SC, dtype=jnp.int32)[None, :] * STEP + offsets[:, :, 1].astype(jnp.int32)).reshape(SR * SC).astype(jnp.int32)
    amplitude = jnp.sqrt(jnp.maximum(patterns - background, 0.0)).reshape(SR * SC, K, K)
    for sweep in range(ITERS):
        padded = jnp.pad(object_field, ((0, 0), (margin, margin), (margin, margin)))
        illumination = probe_wave[0] * probe_wave[0] + probe_wave[1] * probe_wave[1]

        def visit(carry, position_item):
            intersection, gradient = carry
            row_start, col_start, amp_one = position_item
            row_start = row_start.astype(jnp.int32)
            col_start = col_start.astype(jnp.int32)
            channel_zero = jnp.int32(0)
            window = lax.dynamic_slice(padded, (channel_zero, row_start, col_start), (2, K, K))
            exit_wave = product(probe_wave, window)
            far_field = transform(exit_wave.astype(jnp.bfloat16), forward[0], forward[1])
            magnitude = jnp.sqrt(far_field[0] * far_field[0] + far_field[1] * far_field[1])
            projected = (far_field * (amp_one / jnp.maximum(magnitude, 0.5))[None]).astype(jnp.bfloat16)
            back_wave = transform(projected, inverse[0], inverse[1])
            difference = back_wave - exit_wave
            obj_term = jnp.concatenate([times_conj(probe_wave, difference), illumination[None]], axis=0)
            current = lax.dynamic_slice(intersection, (channel_zero, row_start, col_start), (3, K, K))
            intersection = lax.dynamic_update_slice(intersection, current + obj_term, (channel_zero, row_start, col_start))
            return ((intersection, gradient + times_conj(window, difference)), None)
        initial = (jnp.zeros((3, NR + K, NC + K), jnp.float32), jnp.zeros((2, K, K), jnp.float32))
        (intersection, gradient), _ = lax.scan(visit, initial, (start_rows, start_cols, amplitude))
        inner = intersection[:, margin:margin + NR, margin:margin + NC]
        new_object = object_field + inner[0:2] / (inner[2] + 1.0)
        spread = jnp.sqrt(jnp.mean(gradient * gradient) + 1e-06)
        probe_wave = probe_wave + gradient / spread
        object_field = new_object
    return (object_field, probe_wave)
```

```python
import math

import jax
import jax.numpy as jnp
import numpy as np
from jax import lax
from jax.experimental import pallas as pl
from jax.experimental.pallas import tpu as pltpu
from jax.sharding import Mesh, PartitionSpec as P

STEP = 64
ITERS = 2
ROW = ("x", "yl")
COL = ("z", "yh", "core")
NEAR = ("x", "yl", "yh", "core")
CHUNK = 32
f32 = jnp.float32
bf16 = jnp.bfloat16


def dft_tables(side_len):
    index = np.arange(side_len)
    angles = (np.outer(index, index) % side_len).astype(np.float32) * np.float32(
        2.0 * math.pi / side_len
    )
    scaling = np.float32(1.0 / math.sqrt(side_len))
    real = np.cos(angles) * scaling
    imag = -np.sin(angles) * scaling
    first = np.block([[real, -imag], [imag, real]]).astype(bf16)
    second = np.block([[real, imag], [-imag, real]]).astype(bf16)
    return first, second


def shift_from(value, axis, step):
    count = lax.axis_size(axis)
    if step > 0:
        pairs = [(i, i + step) for i in range(count - step)]
    else:
        pairs = [(i, i + step) for i in range(-step, count)]
    return lax.ppermute(value, axis, pairs)


def update_kernel(renew, starts, left, mid, right, amplitude, probe_in, summed, first, second,
                  acc_l, acc_m, acc_r, grad, probe, window, wave, field, bent):
    side = probe.shape[-1]
    count = amplitude.shape[0]
    chunks = side // CHUNK
    if renew:
        square = jnp.zeros((8, side), f32)
        for c in range(2):
            part = summed[c] * summed[c]
            square = square + jnp.sum(part.reshape(side // 8, 8, side), axis=0)
        spread = jnp.sqrt(jnp.sum(square) / (2.0 * side * side) + 1e-06)
        probe[...] = probe_in[...] + summed[...] / spread
    else:
        probe[...] = probe_in[...]
    for ref in (acc_l, acc_m, acc_r):
        ref[...] = jnp.zeros_like(ref)
    for p in range(count):
        row_start = starts[p, 0]
        col_start = starts[p, 1]

        def load(i, _):
            here = pl.ds(pl.multiple_of(i * CHUNK, CHUNK), CHUNK)
            there = pl.ds(row_start + i * CHUNK, CHUNK)
            cut = []
            for c in range(2):
                wide = jnp.concatenate([left[c, there, :], mid[c, there, :], right[c, there, :]], axis=1)
                part = pltpu.roll(wide, 3 * 128 - col_start, 1)[:, :side]
                window[c, here, :] = part
                cut.append(part)
            pr, pi = probe[0, here, :], probe[1, here, :]
            er = pr * cut[0] - pi * cut[1]
            ei = pr * cut[1] + pi * cut[0]
            wave[0, here, :] = er
            wave[1, here, :] = ei
            bent[here, :] = er.astype(bf16)
            bent[pl.ds(pl.multiple_of(side + i * CHUNK, CHUNK), CHUNK), :] = ei.astype(bf16)
            return 0

        lax.fori_loop(0, chunks, load, 0)
        half = jnp.dot(first[...], bent[...], preferred_element_type=f32).astype(bf16)
        half = jnp.concatenate([half[:side], half[side:]], axis=1)
        field[...] = jnp.dot(half, second[...], preferred_element_type=f32)

        def project(i, _):
            here = pl.ds(pl.multiple_of(i * CHUNK, CHUNK), CHUNK)
            fr, fi = field[here, :side], field[here, side:]
            scale = amplitude[p, here, :] * lax.rsqrt(jnp.maximum(fr * fr + fi * fi, 0.25))
            bent[here, :] = (fr * scale).astype(bf16)
            bent[pl.ds(pl.multiple_of(side + i * CHUNK, CHUNK), CHUNK), :] = (fi * scale).astype(bf16)
            return 0

        lax.fori_loop(0, chunks, project, 0)
        half = jnp.dot(second[...], bent[...], preferred_element_type=f32).astype(bf16)
        half = jnp.concatenate([half[:side], half[side:]], axis=1)
        field[...] = jnp.dot(half, first[...], preferred_element_type=f32)

        def spread_out(i, _):
            here = pl.ds(pl.multiple_of(i * CHUNK, CHUNK), CHUNK)
            there = pl.ds(row_start + i * CHUNK, CHUNK)
            dr = field[here, :side] - wave[0, here, :]
            di = field[here, side:] - wave[1, here, :]
            pr, pi = probe[0, here, :], probe[1, here, :]
            wr, wi = window[0, here, :], window[1, here, :]
            gr = wr * dr + wi * di
            gi = wr * di - wi * dr
            if p == 0:
                grad[0, here, :] = gr
                grad[1, here, :] = gi
            else:
                grad[0, here, :] += gr
                grad[1, here, :] += gi
            terms = (pr * dr + pi * di, pr * di - pi * dr, pr * pr + pi * pi)
            for c, term in enumerate(terms):
                wide = jnp.concatenate([term, jnp.zeros((CHUNK, 128), f32)], axis=1)
                moved = pltpu.roll(wide, col_start, 1)
                acc_l[c, there, :] += moved[:, :128]
                acc_m[c, there, :] += moved[:, 128:256]
                acc_r[c, there, :] += moved[:, 256:]
            return 0

        lax.fori_loop(0, chunks, spread_out, 0)


def update(renew, starts, strips, amplitude, probe, summed, tables):
    side = probe.shape[-1]
    strip = jax.ShapeDtypeStruct((3,) + strips[0].shape[1:], f32)
    wave = jax.ShapeDtypeStruct(probe.shape, f32)
    vmem = pl.BlockSpec(memory_space=pltpu.VMEM)
    return pl.pallas_call(
        lambda *refs: update_kernel(renew, *refs),
        out_shape=(strip, strip, strip, wave, wave),
        in_specs=[pl.BlockSpec(memory_space=pltpu.SMEM)] + [vmem] * 8,
        out_specs=(vmem,) * 5,
        scratch_shapes=[
            pltpu.VMEM((2, side, side), f32),
            pltpu.VMEM((2, side, side), f32),
            pltpu.VMEM((side, 2 * side), f32),
            pltpu.VMEM((2 * side, side), bf16),
        ],
        compiler_params=pltpu.CompilerParams(vmem_limit_bytes=40 * 1024 * 1024),
        cost_estimate=pl.CostEstimate(
            flops=amplitude.shape[0] * 32 * side**3, bytes_accessed=8 * 2**20, transcendentals=0
        ),
        name="update",
    )(starts, *strips, amplitude, probe, summed, *tables)


def finish_kernel(probe, summed, out):
    side = probe.shape[-1]
    square = jnp.zeros((8, side), f32)
    for c in range(2):
        part = summed[c] * summed[c]
        square = square + jnp.sum(part.reshape(side // 8, 8, side), axis=0)
    spread = jnp.sqrt(jnp.sum(square) / (2.0 * side * side) + 1e-06)
    out[...] = probe[...] + summed[...] / spread


def finish(probe, summed):
    vmem = pl.BlockSpec(memory_space=pltpu.VMEM)
    return pl.pallas_call(
        finish_kernel,
        out_shape=jax.ShapeDtypeStruct(probe.shape, f32),
        in_specs=[vmem, vmem],
        out_specs=vmem,
        name="finish",
    )(probe, summed)


def total(value):
    near = math.prod(lax.axis_size(a) for a in NEAR)
    flat = value.reshape(near, -1, value.shape[-1])
    part = jnp.sum(lax.all_to_all(flat, NEAR, 0, 0), axis=0)
    deep = lax.axis_size("z")
    part = jnp.sum(lax.all_to_all(jnp.broadcast_to(part, (deep,) + part.shape), "z", 0, 0), axis=0)
    full = lax.all_to_all(jnp.broadcast_to(part, (near,) + part.shape), NEAR, 0, 0)
    return full.reshape(value.shape)


def widen(tile):
    above = shift_from(tile, ROW, 1)
    below = shift_from(tile, ROW, -1)
    tall = jnp.concatenate([above, tile, below], axis=1)
    return (shift_from(tall, COL, 1), tall, shift_from(tall, COL, -1))


def fold(acc_l, acc_m, acc_r):
    length = acc_m.shape[1] // 3
    tall = acc_m + shift_from(acc_r, COL, 1) + shift_from(acc_l, COL, -1)
    top, centre, bottom = (tall[:, i * length : (i + 1) * length] for i in range(3))
    return centre + shift_from(bottom, ROW, 1) + shift_from(top, ROW, -1)


def on_device(patterns, background, offsets, probe, tile):
    side = probe.shape[-1]
    rows, cols = patterns.shape[:2]
    steps = jnp.stack(jnp.meshgrid(jnp.arange(rows), jnp.arange(cols), indexing="ij"), axis=-1)
    starts = (offsets + steps.astype(jnp.int32) * STEP).reshape(rows * cols, 2)
    amplitude = jnp.sqrt(jnp.maximum(patterns.reshape(rows * cols, side, side) - background, 0.0))
    tables = tuple(jnp.asarray(t) for t in dft_tables(side))
    summed = probe
    for step in range(ITERS):
        strips = widen(tile)
        acc_l, acc_m, acc_r, grad, probe = update(
            step > 0, starts, strips, amplitude, probe, summed, tables
        )
        folded = fold(acc_l, acc_m, acc_r)
        tile = tile + folded[0:2] / (folded[2] + 1.0)
        summed = total(grad)
    return tile, finish(probe, summed)


def solution(mesh):
    fine = Mesh(mesh.devices.reshape(4, 2, 8, 2, 2), ROW + COL)
    return jax.shard_map(
        on_device,
        mesh=fine,
        in_specs=(P(ROW, COL, None, None), P(), P(ROW, COL, None), P(), P(None, ROW, COL)),
        out_specs=(P(None, ROW, COL), P()),
        check_vma=False,
    )
```

```python
import math

import jax
import jax.numpy as jnp
import numpy as np
from jax import lax
from jax.experimental import pallas as pl
from jax.experimental.pallas import tpu as pltpu
from jax.sharding import Mesh, PartitionSpec as P

STEP = 64
ITERS = 2
ROW = ("x", "yl")
COL = ("z", "yh", "core")
PLANE = ("x", "yl", "yh")
CHUNK = 256
UNROLL = 1
VMEM_LIMIT = 14 * 1024 * 1024
SMALL = 8 * 1024 * 1024
f32 = jnp.float32
bf16 = jnp.bfloat16
VMEM = pl.BlockSpec(memory_space=pltpu.VMEM)
HBM = pl.BlockSpec(memory_space=pltpu.HBM)
ANY = pl.BlockSpec(memory_space=pl.ANY)
SMEM = pl.BlockSpec(memory_space=pltpu.SMEM)


def dft_table(side_len):
    index = np.arange(side_len)
    angles = (np.outer(index, index) % side_len).astype(np.float32) * np.float32(
        2.0 * math.pi / side_len
    )
    scaling = np.float32(1.0 / math.sqrt(side_len))
    real = np.cos(angles) * scaling
    imag = -np.sin(angles) * scaling
    return np.concatenate([real, imag], axis=1).astype(bf16)


def call(kernel, out_shape, operands, name, scratch=(), scalars=1, flops=0, limit=SMALL, after=()):
    many = isinstance(out_shape, (tuple, list))
    moved = sum(math.prod(o.shape) * o.dtype.itemsize for o in operands)
    waits = len(after)

    def body(*refs):
        kernel(*refs[waits:])

    operands = (*after, *operands)
    return pl.pallas_call(
        body,
        out_shape=out_shape,
        in_specs=[ANY] * waits
        + [SMEM] * scalars
        + [VMEM] * (len(operands) - scalars - waits),
        out_specs=[VMEM] * len(out_shape) if many else VMEM,
        scratch_shapes=list(scratch),
        compiler_params=pltpu.CompilerParams(vmem_limit_bytes=limit),
        cost_estimate=pl.CostEstimate(flops=flops, bytes_accessed=moved, transcendentals=0),
        name=name,
    )(*operands)


def shape(*dims):
    return jax.ShapeDtypeStruct(dims, f32)


def pair_swap(value, axis, first):
    count = lax.axis_size(axis)
    pairs = []
    for i in range(first, count - 1, 2):
        pairs += [(i, i + 1), (i + 1, i)]
    return lax.ppermute(value, axis, pairs)


def renewed(probe, own, other, core, out):
    side = probe.shape[-1]
    square = jnp.zeros((8, side), f32)
    for part in (own, other):
        part = part[...]
        square = square + jnp.sum((part * part).reshape(side // 8, 8, side), axis=0)
    spread = jnp.sqrt(jnp.sum(square) / (2.0 * side * side) + 1e-06)
    scale = jnp.full((8, side), 1.0, f32) / spread
    scale = jnp.broadcast_to(scale[None], (side // 8, 8, side)).reshape(side, side)
    out[core] = probe[core] + own[...] * scale
    out[1 - core] = probe[1 - core] + other[...] * scale


def update_kernel(renew, ids, starts, own, other, sib, mid, cross, amplitude_in, probe_in, table_in,
                  mid_out, keep, give, probe_out, sib_out, cross_out,
                  strips, amplitude, probe, table, first, second, acc, grad, window, wave, field, bent, sems):
    side = probe.shape[-1]
    count = amplitude.shape[0]
    chunks = side // CHUNK
    core = ids[0]
    near, far = 2 * (1 - core), 2 * core
    tall = pl.ds(0, side + side // 2)
    moves = [
        pltpu.make_async_copy(a, b, sems.at[n])
        for n, (a, b) in enumerate((
            (probe_in, probe),
            (mid.at[:, tall], strips.at[1]),
            (sib.at[:, tall], strips.at[near]),
            (cross.at[:, tall], strips.at[far]),
            (table_in, table),
            (amplitude_in, amplitude),
            (acc.at[near], sib_out),
            (acc.at[far], cross_out),
        ))
    ]
    for move in moves[:6]:
        move.start()
    acc[...] = jnp.zeros_like(acc)
    moves[0].wait()
    if renew:
        renewed(probe, own, other, core, probe)
    probe_out[...] = probe[...]
    for move in moves[1:4]:
        move.wait()
    for p in range(count):
        row_start = starts[p, 0]
        col_start = starts[p, 1]

        def load(i, _):
            here = pl.ds(pl.multiple_of(i * CHUNK, CHUNK), CHUNK)
            there = pl.ds(row_start + i * CHUNK, CHUNK)
            cut = []
            for c in range(2):
                wide = jnp.concatenate([strips[k, c, there, :] for k in range(3)], axis=1)
                part = pltpu.roll(wide, 3 * 128 - col_start, 1)[:, :side]
                window[c, here, :] = part
                cut.append(part)
            pr, pi = probe[0, here, :], probe[1, here, :]
            er = pr * cut[0] - pi * cut[1]
            ei = pr * cut[1] + pi * cut[0]
            wave[0, here, :] = er
            wave[1, here, :] = ei
            bent[here, :] = er.astype(bf16)
            bent[pl.ds(pl.multiple_of(side + i * CHUNK, CHUNK), CHUNK), :] = ei.astype(bf16)
            return 0

        lax.fori_loop(0, chunks, load, 0, unroll=UNROLL)
        if p == 0:
            for move in moves[4:6]:
                move.wait()
            real, imag = table[:, :side], table[:, side:]
            first[:side, :side] = real
            first[:side, side:] = -imag
            first[side:, :side] = imag
            first[side:, side:] = real
            second[:side, :side] = real
            second[:side, side:] = imag
            second[side:, :side] = -imag
            second[side:, side:] = real
        half = jnp.dot(first[...], bent[...], preferred_element_type=f32).astype(bf16)
        half = jnp.concatenate([half[:side], half[side:]], axis=1)
        field[...] = jnp.dot(half, second[...], preferred_element_type=f32)

        def project(i, _):
            here = pl.ds(pl.multiple_of(i * CHUNK, CHUNK), CHUNK)
            fr, fi = field[here, :side], field[here, side:]
            scale = amplitude[p, here, :] * lax.rsqrt(jnp.maximum(fr * fr + fi * fi, 0.25))
            bent[here, :] = (fr * scale).astype(bf16)
            bent[pl.ds(pl.multiple_of(side + i * CHUNK, CHUNK), CHUNK), :] = (fi * scale).astype(bf16)
            return 0

        lax.fori_loop(0, chunks, project, 0, unroll=UNROLL)
        half = jnp.dot(second[...], bent[...], preferred_element_type=f32).astype(bf16)
        half = jnp.concatenate([half[:side], half[side:]], axis=1)
        field[...] = jnp.dot(half, first[...], preferred_element_type=f32)

        def spread_out(i, _):
            here = pl.ds(pl.multiple_of(i * CHUNK, CHUNK), CHUNK)
            there = pl.ds(row_start + i * CHUNK, CHUNK)
            dr = field[here, :side] - wave[0, here, :]
            di = field[here, side:] - wave[1, here, :]
            pr, pi = probe[0, here, :], probe[1, here, :]
            wr, wi = window[0, here, :], window[1, here, :]
            gr = wr * dr + wi * di
            gi = wr * di - wi * dr
            if p > 0:
                gr = gr + grad[0, here, :]
                gi = gi + grad[1, here, :]
            if p < count - 1:
                grad[0, here, :] = gr
                grad[1, here, :] = gi
            else:
                keep[here, :] = jnp.where(core == 0, gr, gi)
                give[here, :] = jnp.where(core == 0, gi, gr)
            terms = (pr * dr + pi * di, pr * di - pi * dr)
            for c, term in enumerate(terms):
                wide = jnp.concatenate([term, jnp.zeros((CHUNK, 128), f32)], axis=1)
                moved = pltpu.roll(wide, col_start, 1)
                for k in range(3):
                    acc[k, c, there, :] += moved[:, 128 * k : 128 * (k + 1)]
            return 0

        lax.fori_loop(0, chunks, spread_out, 0, unroll=UNROLL)
    moves[6].start()
    moves[7].start()
    mid_out[...] = acc[1]
    for move in moves[6:]:
        move.wait()


def update(renew, ids, starts, parts, amplitude, probe, own, other, table):
    side = probe.shape[-1]
    rows, cols = side + side // 2, parts[0].shape[2]
    strip, square, wave = shape(2, rows, cols), shape(side, side), shape(2, side, side)
    count = amplitude.shape[0]
    return pl.pallas_call(
        lambda *refs: update_kernel(renew, *refs),
        out_shape=(strip, square, square, wave, strip, strip),
        in_specs=[SMEM] * 2 + [VMEM] * 2 + [HBM] * 6,
        out_specs=[VMEM] * 4 + [HBM] * 2,
        scratch_shapes=(
            pltpu.VMEM((3, 2, rows, cols), f32),
            pltpu.VMEM((count, side, side), f32),
            pltpu.VMEM((2, side, side), f32),
            pltpu.VMEM((side, 2 * side), bf16),
            pltpu.VMEM((2 * side, 2 * side), bf16),
            pltpu.VMEM((2 * side, 2 * side), bf16),
            pltpu.VMEM((3, 2, rows, cols), f32),
            pltpu.VMEM((2, side, side), f32),
            pltpu.VMEM((2, side, side), f32),
            pltpu.VMEM((2, side, side), f32),
            pltpu.VMEM((side, 2 * side), f32),
            pltpu.VMEM((2 * side, side), bf16),
            pltpu.SemaphoreType.DMA((8,)),
        ),
        compiler_params=pltpu.CompilerParams(vmem_limit_bytes=VMEM_LIMIT),
        cost_estimate=pl.CostEstimate(
            flops=count * 64 * side**3, bytes_accessed=0, transcendentals=0
        ),
        name="update",
    )(ids, starts, own, other, *parts, amplitude, probe, table)


def hold(value, after):
    return pl.pallas_call(
        lambda *refs: None,
        out_shape=jax.ShapeDtypeStruct(value.shape, value.dtype),
        in_specs=[ANY, ANY],
        out_specs=ANY,
        input_output_aliases={0: 0},
        name="hold",
    )(value, after)


def finish(ids, probe, own, other):
    def kernel(ids, probe, own, other, out):
        renewed(probe, own, other, ids[0], out)

    return call(kernel, shape(*probe.shape), (ids, probe, own, other), "finish")


def sum_and_repeat(value, copies, after):
    def kernel(value, out):
        added = value[0]
        for i in range(1, value.shape[0]):
            added = added + value[i]
        for i in range(copies):
            out[i] = added

    return call(kernel, shape(copies, *value.shape[1:]), (value,), "sum_repeat", scalars=0, after=after)


def add_into_ways(a, b, ways):
    return (a + b).reshape(ways, -1, a.shape[-1])


def scatter(keep, give):
    plane = math.prod(lax.axis_size(a) for a in PLANE)
    return lax.all_to_all(add_into_ways(keep, pair_swap(give, "core", 0), plane), PLANE, 0, 0)


def gather(part, first, second, third=None):
    plane = part.shape[0]
    part = sum_and_repeat(part, lax.axis_size("z"), first)
    part = sum_and_repeat(lax.all_to_all(part, "z", 0, 0), plane, second)
    own = lax.all_to_all(part, PLANE, 0, 0).reshape(-1, part.shape[-1])
    if third is not None:
        own = hold(own, third)
    return own, pair_swap(own, "core", 0)


def widen(ids, tile):
    channels, rows, cols = tile.shape
    side = cols
    tags = rows - side

    def kernel(ids, near, tile, far, out):
        flip = ids[1]
        for ref, place in ((near, 2 * (1 - flip)), (tile, 1), (far, 2 * flip)):
            out[:, pl.ds(pl.multiple_of(side * place, side), side), :] = ref[:, :side, :]
            if tags:
                there = pl.ds(pl.multiple_of(3 * side + tags * place, tags), tags)
                out[:, there, :] = ref[:, side:, :]

    far = pair_swap(tile, ROW, 1)
    near = pair_swap(tile, ROW, 0)
    tall = call(kernel, shape(channels, 3 * rows, cols), (ids, near, tile, far), "stack")
    return pair_swap(tall, COL, 0), tall, pair_swap(tall, COL, 1)


def light(ids, spots, probe):
    side = probe.shape[-1]
    half = side // 2

    def kernel(ids, spots, probe, out, pad):
        core = ids[0]
        bright = probe[0] * probe[0] + probe[1] * probe[1]
        pad[...] = jnp.zeros_like(pad)
        pad[1, half : half + side, :] = bright[:, :half]
        pad[2, half : half + side, :] = bright[:, half:]
        added = jnp.zeros((half, half), f32)
        for k, beside in enumerate((1 - 2 * core, 0, 2 * core - 1)):
            for r in range(3):
                for p in range(spots.shape[2] // 2):
                    tag = spots[k, r, 2 * p]
                    u = jnp.where(tag > 0, side + 1 - tag - (r - 1) * half, 0)
                    v = side + 1 - spots[k, r, 2 * p + 1] - beside * half
                    v = jnp.where(tag > 0, v, 0)
                    lane = jnp.bitwise_and(v, half - 1)
                    block = lax.div(v, half)
                    here = pl.ds(u, half)
                    wide = jnp.concatenate([pad[block, here, :], pad[block + 1, here, :]], axis=1)
                    moved = pltpu.roll(wide, jnp.bitwise_and(side - lane, side - 1), 1)
                    added = added + moved[:, :half]
        out[...] = added

    return call(
        kernel,
        shape(half, half),
        (ids, spots, probe),
        "light",
        scratch=(pltpu.VMEM((5, 2 * side, half), f32),),
        scalars=2,
        flops=2 * 10**9,
    )


def fold(ids, tile, bright, sib, mid, cross):
    channels, tall, cols = mid.shape
    rows = tall // 3

    def split(ids, mid, sib, cross, near, own, far):
        flip = ids[1]

        def part(start):
            here = pl.ds(start, rows)
            return mid[:, here, :] + sib[:, here, :] + cross[:, here, :]

        near[...] = part(pl.multiple_of(2 * rows * (1 - flip), rows))
        own[...] = part(rows)
        far[...] = part(pl.multiple_of(2 * rows * flip, rows))

    def renew(tile, bright, near, own, far, out):
        part = near[...] + own[...] + far[...]
        out[...] = tile[...] + part / (bright[...] + 1.0)

    cross = pair_swap(cross, COL, 1)
    sib = pair_swap(sib, COL, 0)
    near, own, far = call(split, [shape(channels, rows, cols)] * 3, (ids, mid, sib, cross), "split")
    far = pair_swap(far, ROW, 1)
    near = pair_swap(near, ROW, 0)
    return own, call(renew, shape(*tile.shape), (tile, bright, near, own, far), "renew", scalars=0)


def on_device(patterns, background, offsets, probe, tile):
    side = probe.shape[-1]
    rows, cols = patterns.shape[:2]
    steps = jnp.stack(jnp.meshgrid(jnp.arange(rows), jnp.arange(cols), indexing="ij"), axis=-1)
    starts = (offsets + steps.astype(jnp.int32) * STEP).reshape(rows * cols, 2)
    ids = jnp.stack([lax.axis_index("core"), lax.axis_index("yl")]).astype(jnp.int32)
    amplitude = jnp.sqrt(jnp.maximum(patterns.reshape(rows * cols, side, side) - background, 0.0))
    table = jnp.asarray(dft_table(side))
    own = other = background
    tags = starts.reshape(1, 1, 2 * rows * cols).astype(f32) + 1.0
    tags = jnp.pad(tags, ((0, 0), (0, 7), (0, tile.shape[2] - tags.shape[2])))
    tags = jnp.broadcast_to(tags, (2,) + tags.shape[1:])
    parts = widen(ids, jnp.concatenate([tile, tags], axis=1))
    tall = side + side // 2
    spots = jnp.stack([v[0, tall::8, : 2 * rows * cols] for v in parts]).astype(jnp.int32)
    for step in range(ITERS):
        mid, keep, give, new_probe, sib, cross = update(
            step > 0, ids, starts, parts, amplitude, probe, own, other, table
        )
        if step > 0:
            probe = new_probe
        bright = light(ids, spots, probe)
        part = scatter(keep, give)
        last = step == ITERS - 1
        if last:
            cross = hold(cross, part)
        centre, tile = fold(ids, tile, bright, sib, mid, cross)
        if last:
            own, other = gather(part, (), (centre,), tile)
        else:
            parts = widen(ids, tile)
            own, other = gather(part, (tile,), (parts[1],))
    return tile, finish(ids, probe, own, other)


def solution(mesh):
    fine = Mesh(mesh.devices.reshape(4, 2, 8, 2, 2), ROW + COL)
    return jax.shard_map(
        on_device,
        mesh=fine,
        in_specs=(P(ROW, COL, None, None), P(), P(ROW, COL, None), P(), P(None, ROW, COL)),
        out_specs=(P(None, ROW, COL), P()),
        check_vma=False,
    )
```

```python
import math

import jax
import jax.numpy as jnp
import numpy as np
from jax import lax
from jax.experimental import pallas as pl
from jax.experimental.pallas import tpu as pltpu
from jax.sharding import Mesh, PartitionSpec as P

STEP = 64
ITERS = 2
ROW = ("x", "yl")
COL = ("z", "yh", "core")
PLANE = ("x", "yl", "yh")
CHUNK = 256
UNROLL = 1
VMEM_LIMIT = 14 * 1024 * 1024
SMALL = 8 * 1024 * 1024
f32 = jnp.float32
bf16 = jnp.bfloat16
VMEM = pl.BlockSpec(memory_space=pltpu.VMEM)
HBM = pl.BlockSpec(memory_space=pltpu.HBM)
ANY = pl.BlockSpec(memory_space=pl.ANY)
SMEM = pl.BlockSpec(memory_space=pltpu.SMEM)


def dft_table(side_len):
    index = np.arange(side_len)
    angles = (np.outer(index, index) % side_len).astype(np.float32) * np.float32(
        2.0 * math.pi / side_len
    )
    scaling = np.float32(1.0 / math.sqrt(side_len))
    real = np.cos(angles) * scaling
    imag = -np.sin(angles) * scaling
    return np.concatenate([real, imag], axis=1).astype(bf16)


def call(kernel, out_shape, operands, name, scratch=(), scalars=1, flops=0, limit=SMALL, after=()):
    many = isinstance(out_shape, (tuple, list))
    moved = sum(math.prod(o.shape) * o.dtype.itemsize for o in operands)
    waits = len(after)

    def body(*refs):
        kernel(*refs[waits:])

    operands = (*after, *operands)
    return pl.pallas_call(
        body,
        out_shape=out_shape,
        in_specs=[ANY] * waits
        + [SMEM] * scalars
        + [VMEM] * (len(operands) - scalars - waits),
        out_specs=[VMEM] * len(out_shape) if many else VMEM,
        scratch_shapes=list(scratch),
        compiler_params=pltpu.CompilerParams(vmem_limit_bytes=limit),
        cost_estimate=pl.CostEstimate(flops=flops, bytes_accessed=moved, transcendentals=0),
        name=name,
    )(*operands)


def shape(*dims):
    return jax.ShapeDtypeStruct(dims, f32)


def pair_swap(value, axis, first):
    count = lax.axis_size(axis)
    pairs = []
    for i in range(first, count - 1, 2):
        pairs += [(i, i + 1), (i + 1, i)]
    return lax.ppermute(value, axis, pairs)


def renewed(probe, own, other, core, out):
    side = probe.shape[-1]
    square = jnp.zeros((8, side), f32)
    for part in (own, other):
        part = part[...]
        square = square + jnp.sum((part * part).reshape(side // 8, 8, side), axis=0)
    spread = jnp.sqrt(jnp.sum(square) / (2.0 * side * side) + 1e-06)
    scale = jnp.full((8, side), 1.0, f32) / spread
    scale = jnp.broadcast_to(scale[None], (side // 8, 8, side)).reshape(side, side)
    out[core] = probe[core] + own[...] * scale
    out[1 - core] = probe[1 - core] + other[...] * scale


def update_kernel(renew, ids, starts, own, other, sib, mid, cross, amplitude_in, probe_in, table_in,
                  mid_out, keep, give, probe_out, sib_out, cross_out,
                  strips, amplitude, probe, table, first, second, acc, grad, window, wave, field, bent, sems):
    side = probe.shape[-1]
    count = amplitude.shape[0]
    chunks = side // CHUNK
    core = ids[0]
    near, far = 2 * (1 - core), 2 * core
    tall = pl.ds(0, side + side // 2)
    moves = [
        pltpu.make_async_copy(a, b, sems.at[n])
        for n, (a, b) in enumerate((
            (probe_in, probe),
            (mid.at[:, tall], strips.at[1]),
            (sib.at[:, tall], strips.at[near]),
            (cross.at[:, tall], strips.at[far]),
            (table_in, table),
            (amplitude_in, amplitude),
            (acc.at[near], sib_out),
            (acc.at[far], cross_out),
        ))
    ]
    for move in moves[:6]:
        move.start()
    acc[...] = jnp.zeros_like(acc)
    moves[0].wait()
    if renew:
        renewed(probe, own, other, core, probe)
    probe_out[...] = probe[...]
    for move in moves[1:4]:
        move.wait()
    for p in range(count):
        row_start = starts[p, 0]
        col_start = starts[p, 1]

        def load(i, _):
            here = pl.ds(pl.multiple_of(i * CHUNK, CHUNK), CHUNK)
            there = pl.ds(row_start + i * CHUNK, CHUNK)
            cut = []
            for c in range(2):
                wide = jnp.concatenate([strips[k, c, there, :] for k in range(3)], axis=1)
                part = pltpu.roll(wide, 3 * 128 - col_start, 1)[:, :side]
                window[c, here, :] = part
                cut.append(part)
            pr, pi = probe[0, here, :], probe[1, here, :]
            er = pr * cut[0] - pi * cut[1]
            ei = pr * cut[1] + pi * cut[0]
            wave[0, here, :] = er
            wave[1, here, :] = ei
            bent[here, :] = er.astype(bf16)
            bent[pl.ds(pl.multiple_of(side + i * CHUNK, CHUNK), CHUNK), :] = ei.astype(bf16)
            return 0

        lax.fori_loop(0, chunks, load, 0, unroll=UNROLL)
        if p == 0:
            for move in moves[4:6]:
                move.wait()
            real, imag = table[:, :side], table[:, side:]
            first[:side, :side] = real
            first[:side, side:] = -imag
            first[side:, :side] = imag
            first[side:, side:] = real
            second[:side, :side] = real
            second[:side, side:] = imag
            second[side:, :side] = -imag
            second[side:, side:] = real
        half = jnp.dot(first[...], bent[...], preferred_element_type=f32).astype(bf16)
        half = jnp.concatenate([half[:side], half[side:]], axis=1)
        field[...] = jnp.dot(half, second[...], preferred_element_type=f32)

        def project(i, _):
            here = pl.ds(pl.multiple_of(i * CHUNK, CHUNK), CHUNK)
            fr, fi = field[here, :side], field[here, side:]
            scale = amplitude[p, here, :] * lax.rsqrt(jnp.maximum(fr * fr + fi * fi, 0.25))
            bent[here, :] = (fr * scale).astype(bf16)
            bent[pl.ds(pl.multiple_of(side + i * CHUNK, CHUNK), CHUNK), :] = (fi * scale).astype(bf16)
            return 0

        lax.fori_loop(0, chunks, project, 0, unroll=UNROLL)
        half = jnp.dot(second[...], bent[...], preferred_element_type=f32).astype(bf16)
        half = jnp.concatenate([half[:side], half[side:]], axis=1)
        field[...] = jnp.dot(half, first[...], preferred_element_type=f32)

        def spread_out(i, _):
            here = pl.ds(pl.multiple_of(i * CHUNK, CHUNK), CHUNK)
            there = pl.ds(row_start + i * CHUNK, CHUNK)
            dr = field[here, :side] - wave[0, here, :]
            di = field[here, side:] - wave[1, here, :]
            pr, pi = probe[0, here, :], probe[1, here, :]
            wr, wi = window[0, here, :], window[1, here, :]
            gr = wr * dr + wi * di
            gi = wr * di - wi * dr
            if p > 0:
                gr = gr + grad[0, here, :]
                gi = gi + grad[1, here, :]
            if p < count - 1:
                grad[0, here, :] = gr
                grad[1, here, :] = gi
            else:
                keep[here, :] = jnp.where(core == 0, gr, gi)
                give[here, :] = jnp.where(core == 0, gi, gr)
            terms = (pr * dr + pi * di, pr * di - pi * dr)
            for c, term in enumerate(terms):
                wide = jnp.concatenate([term, jnp.zeros((CHUNK, 128), f32)], axis=1)
                moved = pltpu.roll(wide, col_start, 1)
                for k in range(3):
                    acc[k, c, there, :] += moved[:, 128 * k : 128 * (k + 1)]
            return 0

        lax.fori_loop(0, chunks, spread_out, 0, unroll=UNROLL)
    moves[6].start()
    moves[7].start()
    mid_out[...] = acc[1]
    for move in moves[6:]:
        move.wait()


def update(renew, ids, starts, parts, amplitude, probe, own, other, table):
    side = probe.shape[-1]
    rows, cols = side + side // 2, parts[0].shape[2]
    strip, square, wave = shape(2, rows, cols), shape(side, side), shape(2, side, side)
    count = amplitude.shape[0]
    return pl.pallas_call(
        lambda *refs: update_kernel(renew, *refs),
        out_shape=(strip, square, square, wave, strip, strip),
        in_specs=[SMEM] * 2 + [VMEM] * 2 + [HBM] * 6,
        out_specs=[VMEM] * 4 + [HBM] * 2,
        scratch_shapes=(
            pltpu.VMEM((3, 2, rows, cols), f32),
            pltpu.VMEM((count, side, side), f32),
            pltpu.VMEM((2, side, side), f32),
            pltpu.VMEM((side, 2 * side), bf16),
            pltpu.VMEM((2 * side, 2 * side), bf16),
            pltpu.VMEM((2 * side, 2 * side), bf16),
            pltpu.VMEM((3, 2, rows, cols), f32),
            pltpu.VMEM((2, side, side), f32),
            pltpu.VMEM((2, side, side), f32),
            pltpu.VMEM((2, side, side), f32),
            pltpu.VMEM((side, 2 * side), f32),
            pltpu.VMEM((2 * side, side), bf16),
            pltpu.SemaphoreType.DMA((8,)),
        ),
        compiler_params=pltpu.CompilerParams(vmem_limit_bytes=VMEM_LIMIT),
        cost_estimate=pl.CostEstimate(
            flops=count * 64 * side**3, bytes_accessed=0, transcendentals=0
        ),
        name="update",
    )(ids, starts, own, other, *parts, amplitude, probe, table)


def hold(value, after):
    return pl.pallas_call(
        lambda *refs: None,
        out_shape=jax.ShapeDtypeStruct(value.shape, value.dtype),
        in_specs=[ANY, ANY],
        out_specs=ANY,
        input_output_aliases={0: 0},
        name="hold",
    )(value, after)


def finish(ids, probe, own, other):
    def kernel(ids, probe, own, other, out):
        renewed(probe, own, other, ids[0], out)

    return call(kernel, shape(*probe.shape), (ids, probe, own, other), "finish")


def sum_and_repeat(value, copies, after):
    def kernel(value, out):
        added = value[0]
        for i in range(1, value.shape[0]):
            added = added + value[i]
        for i in range(copies):
            out[i] = added

    return call(kernel, shape(copies, *value.shape[1:]), (value,), "sum_repeat", scalars=0, after=after)


def add_into_ways(a, b, ways):
    return (a + b).reshape(ways, -1, a.shape[-1])


def spread_over(keep, give):
    plane = math.prod(lax.axis_size(a) for a in PLANE)
    return add_into_ways(keep, pair_swap(give, "core", 0), plane)


def widen(ids, tile, after=()):
    channels, rows, cols = tile.shape
    side = cols
    tags = rows - side

    def kernel(ids, near, tile, far, out):
        flip = ids[1]
        for ref, place in ((near, 2 * (1 - flip)), (tile, 1), (far, 2 * flip)):
            out[:, pl.ds(pl.multiple_of(side * place, side), side), :] = ref[:, :side, :]
            if tags:
                there = pl.ds(pl.multiple_of(3 * side + tags * place, tags), tags)
                out[:, there, :] = ref[:, side:, :]

    far = pair_swap(tile, ROW, 1)
    near = pair_swap(tile, ROW, 0)
    tall = call(kernel, shape(channels, 3 * rows, cols), (ids, near, tile, far), "stack", after=after)
    return pair_swap(tall, COL, 0), tall, pair_swap(tall, COL, 1)


def light(ids, spots, probe):
    side = probe.shape[-1]
    half = side // 2

    def kernel(ids, spots, probe, out, pad):
        core = ids[0]
        bright = probe[0] * probe[0] + probe[1] * probe[1]
        pad[...] = jnp.zeros_like(pad)
        pad[1, half : half + side, :] = bright[:, :half]
        pad[2, half : half + side, :] = bright[:, half:]
        added = jnp.zeros((half, half), f32)
        for k, beside in enumerate((1 - 2 * core, 0, 2 * core - 1)):
            for r in range(3):
                for p in range(spots.shape[2] // 2):
                    tag = spots[k, r, 2 * p]
                    u = jnp.where(tag > 0, side + 1 - tag - (r - 1) * half, 0)
                    v = side + 1 - spots[k, r, 2 * p + 1] - beside * half
                    v = jnp.where(tag > 0, v, 0)
                    lane = jnp.bitwise_and(v, half - 1)
                    block = lax.div(v, half)
                    here = pl.ds(u, half)
                    wide = jnp.concatenate([pad[block, here, :], pad[block + 1, here, :]], axis=1)
                    moved = pltpu.roll(wide, jnp.bitwise_and(side - lane, side - 1), 1)
                    added = added + moved[:, :half]
        out[...] = added

    return call(
        kernel,
        shape(half, half),
        (ids, spots, probe),
        "light",
        scratch=(pltpu.VMEM((5, 2 * side, half), f32),),
        scalars=2,
        flops=2 * 10**9,
    )


def split(ids, sib, mid, cross):
    channels, tall, cols = mid.shape
    rows = tall // 3

    def kernel(ids, mid, sib, cross, near, own, far):
        flip = ids[1]

        def part(start):
            here = pl.ds(start, rows)
            return mid[:, here, :] + sib[:, here, :] + cross[:, here, :]

        near[...] = part(pl.multiple_of(2 * rows * (1 - flip), rows))
        own[...] = part(rows)
        far[...] = part(pl.multiple_of(2 * rows * flip, rows))

    cross = pair_swap(cross, COL, 1)
    sib = pair_swap(sib, COL, 0)
    near, own, far = call(kernel, [shape(channels, rows, cols)] * 3, (ids, mid, sib, cross), "split")
    return pair_swap(near, ROW, 0), own, pair_swap(far, ROW, 1)


def renew(tile, bright, near, own, far, after):
    def kernel(tile, bright, near, own, far, out):
        part = near[...] + own[...] + far[...]
        out[...] = tile[...] + part / (bright[...] + 1.0)

    operands = (tile, bright, near, own, far)
    return call(kernel, shape(*tile.shape), operands, "renew", scalars=0, after=after)


def on_device(patterns, background, offsets, probe, tile):
    side = probe.shape[-1]
    rows, cols = patterns.shape[:2]
    steps = jnp.stack(jnp.meshgrid(jnp.arange(rows), jnp.arange(cols), indexing="ij"), axis=-1)
    starts = (offsets + steps.astype(jnp.int32) * STEP).reshape(rows * cols, 2)
    ids = jnp.stack([lax.axis_index("core"), lax.axis_index("yl")]).astype(jnp.int32)
    amplitude = jnp.sqrt(jnp.maximum(patterns.reshape(rows * cols, side, side) - background, 0.0))
    table = jnp.asarray(dft_table(side))
    own = other = background
    tags = starts.reshape(1, 1, 2 * rows * cols).astype(f32) + 1.0
    tags = jnp.pad(tags, ((0, 0), (0, 7), (0, tile.shape[2] - tags.shape[2])))
    tags = jnp.broadcast_to(tags, (2,) + tags.shape[1:])
    parts = widen(ids, jnp.concatenate([tile, tags], axis=1))
    tall = side + side // 2
    spots = jnp.stack([v[0, tall::8, : 2 * rows * cols] for v in parts]).astype(jnp.int32)
    for step in range(ITERS):
        mid, keep, give, new_probe, sib, cross = update(
            step > 0, ids, starts, parts, amplitude, probe, own, other, table
        )
        if step > 0:
            probe = new_probe
        bright = light(ids, spots, probe)
        last = step == ITERS - 1
        part = spread_over(keep, give)
        ways, deep = part.shape[0], lax.axis_size("z")
        if last:
            cross = hold(cross, part)
        near, centre, far = split(ids, sib, mid, cross)
        part = lax.all_to_all(part, PLANE, 0, 0)
        part = sum_and_repeat(part, deep, () if last else (centre,))
        if not last:
            tile = renew(tile, bright, near, centre, far, (part,))
        part = lax.all_to_all(part, "z", 0, 0)
        part = sum_and_repeat(part, ways, (centre,) if last else (tile,))
        if last:
            tile = renew(tile, bright, near, centre, far, ())
        else:
            parts = widen(ids, tile, (part,))
        own = lax.all_to_all(part, PLANE, 0, 0).reshape(side, side)
        other = pair_swap(hold(own, tile) if last else own, "core", 0)
    return tile, finish(ids, probe, own, other)


def solution(mesh):
    fine = Mesh(mesh.devices.reshape(4, 2, 8, 2, 2), ROW + COL)
    return jax.shard_map(
        on_device,
        mesh=fine,
        in_specs=(P(ROW, COL, None, None), P(), P(ROW, COL, None), P(), P(None, ROW, COL)),
        out_specs=(P(None, ROW, COL), P()),
        check_vma=False,
    )
```

```python
import math

import jax
import jax.numpy as jnp
import numpy as np
from jax import lax
from jax.experimental import pallas as pl
from jax.experimental.pallas import tpu as pltpu
from jax.sharding import Mesh, PartitionSpec as P

STEP = 64
ITERS = 2
ROW = ("x", "yl")
COL = ("z", "yh", "core")
PLANE = ("x", "yl", "yh")
CHUNK = 256
UNROLL = 1
VMEM_LIMIT = 14 * 1024 * 1024
SMALL = 8 * 1024 * 1024
f32 = jnp.float32
bf16 = jnp.bfloat16
VMEM = pl.BlockSpec(memory_space=pltpu.VMEM)
HBM = pl.BlockSpec(memory_space=pltpu.HBM)
ANY = pl.BlockSpec(memory_space=pl.ANY)
SMEM = pl.BlockSpec(memory_space=pltpu.SMEM)


def dft_table(side_len):
    index = np.arange(side_len)
    angles = (np.outer(index, index) % side_len).astype(np.float32) * np.float32(
        2.0 * math.pi / side_len
    )
    scaling = np.float32(1.0 / math.sqrt(side_len))
    real = np.cos(angles) * scaling
    imag = -np.sin(angles) * scaling
    return np.concatenate([real, imag], axis=1).astype(bf16)


def call(kernel, out_shape, operands, name, scratch=(), scalars=1, flops=0, limit=SMALL, after=()):
    many = isinstance(out_shape, (tuple, list))
    moved = sum(math.prod(o.shape) * o.dtype.itemsize for o in operands)
    waits = len(after)

    def body(*refs):
        kernel(*refs[waits:])

    operands = (*after, *operands)
    return pl.pallas_call(
        body,
        out_shape=out_shape,
        in_specs=[ANY] * waits
        + [SMEM] * scalars
        + [VMEM] * (len(operands) - scalars - waits),
        out_specs=[VMEM] * len(out_shape) if many else VMEM,
        scratch_shapes=list(scratch),
        compiler_params=pltpu.CompilerParams(vmem_limit_bytes=limit),
        cost_estimate=pl.CostEstimate(flops=flops, bytes_accessed=moved, transcendentals=0),
        name=name,
    )(*operands)


def shape(*dims):
    return jax.ShapeDtypeStruct(dims, f32)


def pair_swap(value, axis, first):
    count = lax.axis_size(axis)
    pairs = []
    for i in range(first, count - 1, 2):
        pairs += [(i, i + 1), (i + 1, i)]
    return lax.ppermute(value, axis, pairs)


def renewed(probe, own, other, core, out):
    side = probe.shape[-1]
    square = jnp.zeros((8, side), f32)
    for part in (own, other):
        part = part[...]
        square = square + jnp.sum((part * part).reshape(side // 8, 8, side), axis=0)
    spread = jnp.sqrt(jnp.sum(square) / (2.0 * side * side) + 1e-06)
    scale = jnp.full((8, side), 1.0, f32) / spread
    scale = jnp.broadcast_to(scale[None], (side // 8, 8, side)).reshape(side, side)
    out[core] = probe[core] + own[...] * scale
    out[1 - core] = probe[1 - core] + other[...] * scale


def update_kernel(renew, ids, starts, own, other, sib, mid, cross, amplitude_in, probe_in, table_in,
                  mid_out, keep, give, probe_out, sib_out, cross_out,
                  strips, amplitude, probe, table, first, second, acc, grad, window, wave, field, bent, sems):
    side = probe.shape[-1]
    count = amplitude.shape[0]
    chunks = side // CHUNK
    core = ids[0]
    near, far = 2 * (1 - core), 2 * core
    tall = pl.ds(0, side + side // 2)
    moves = [
        pltpu.make_async_copy(a, b, sems.at[n])
        for n, (a, b) in enumerate((
            (probe_in, probe),
            (mid.at[:, tall], strips.at[1]),
            (sib.at[:, tall], strips.at[near]),
            (cross.at[:, tall], strips.at[far]),
            (table_in, table),
            (amplitude_in, amplitude),
            (acc.at[near], sib_out),
            (acc.at[far], cross_out),
        ))
    ]
    for move in moves[:6]:
        move.start()
    acc[...] = jnp.zeros_like(acc)
    moves[0].wait()
    if renew:
        renewed(probe, own, other, core, probe)
        probe_out[...] = probe[...]
    else:
        probe_out[...] = jnp.zeros_like(probe_out)
    for move in moves[1:4]:
        move.wait()
    for p in range(count):
        row_start = starts[p, 0]
        col_start = starts[p, 1]

        def load(i, _):
            here = pl.ds(pl.multiple_of(i * CHUNK, CHUNK), CHUNK)
            there = pl.ds(row_start + i * CHUNK, CHUNK)
            cut = []
            for c in range(2):
                wide = jnp.concatenate([strips[k, c, there, :] for k in range(3)], axis=1)
                part = pltpu.roll(wide, 3 * 128 - col_start, 1)[:, :side]
                window[c, here, :] = part
                cut.append(part)
            pr, pi = probe[0, here, :], probe[1, here, :]
            er = pr * cut[0] - pi * cut[1]
            ei = pr * cut[1] + pi * cut[0]
            wave[0, here, :] = er
            wave[1, here, :] = ei
            bent[here, :] = er.astype(bf16)
            bent[pl.ds(pl.multiple_of(side + i * CHUNK, CHUNK), CHUNK), :] = ei.astype(bf16)
            return 0

        lax.fori_loop(0, chunks, load, 0, unroll=UNROLL)
        if p == 0:
            for move in moves[4:6]:
                move.wait()
            real, imag = table[:, :side], table[:, side:]
            first[:side, :side] = real
            first[:side, side:] = -imag
            first[side:, :side] = imag
            first[side:, side:] = real
            second[:side, :side] = real
            second[:side, side:] = imag
            second[side:, :side] = -imag
            second[side:, side:] = real
        half = jnp.dot(first[...], bent[...], preferred_element_type=f32).astype(bf16)
        half = jnp.concatenate([half[:side], half[side:]], axis=1)
        field[...] = jnp.dot(half, second[...], preferred_element_type=f32)

        def project(i, _):
            here = pl.ds(pl.multiple_of(i * CHUNK, CHUNK), CHUNK)
            fr, fi = field[here, :side], field[here, side:]
            scale = amplitude[p, here, :] * lax.rsqrt(jnp.maximum(fr * fr + fi * fi, 0.25))
            bent[here, :] = (fr * scale).astype(bf16)
            bent[pl.ds(pl.multiple_of(side + i * CHUNK, CHUNK), CHUNK), :] = (fi * scale).astype(bf16)
            return 0

        lax.fori_loop(0, chunks, project, 0, unroll=UNROLL)
        half = jnp.dot(second[...], bent[...], preferred_element_type=f32).astype(bf16)
        half = jnp.concatenate([half[:side], half[side:]], axis=1)
        field[...] = jnp.dot(half, first[...], preferred_element_type=f32)

        def spread_out(i, _):
            here = pl.ds(pl.multiple_of(i * CHUNK, CHUNK), CHUNK)
            there = pl.ds(row_start + i * CHUNK, CHUNK)
            dr = field[here, :side] - wave[0, here, :]
            di = field[here, side:] - wave[1, here, :]
            pr, pi = probe[0, here, :], probe[1, here, :]
            wr, wi = window[0, here, :], window[1, here, :]
            gr = wr * dr + wi * di
            gi = wr * di - wi * dr
            if p > 0:
                gr = gr + grad[0, here, :]
                gi = gi + grad[1, here, :]
            if p < count - 1:
                grad[0, here, :] = gr
                grad[1, here, :] = gi
            else:
                keep[here, :] = jnp.where(core == 0, gr, gi)
                give[here, :] = jnp.where(core == 0, gi, gr)
            terms = (pr * dr + pi * di, pr * di - pi * dr)
            for c, term in enumerate(terms):
                wide = jnp.concatenate([term, jnp.zeros((CHUNK, 128), f32)], axis=1)
                moved = pltpu.roll(wide, col_start, 1)
                for k in range(3):
                    acc[k, c, there, :] += moved[:, 128 * k : 128 * (k + 1)]
            return 0

        lax.fori_loop(0, chunks, spread_out, 0, unroll=UNROLL)
    moves[6].start()
    moves[7].start()
    mid_out[...] = acc[1]
    for move in moves[6:]:
        move.wait()


def update(renew, ids, starts, parts, amplitude, probe, own, other, table):
    side = probe.shape[-1]
    rows, cols = side + side // 2, parts[0].shape[2]
    strip, square, wave = shape(2, rows, cols), shape(side, side), shape(2, side, side)
    count = amplitude.shape[0]
    if not renew:
        wave = shape(8, 128)
    return pl.pallas_call(
        lambda *refs: update_kernel(renew, *refs),
        out_shape=(strip, square, square, wave, strip, strip),
        in_specs=[SMEM] * 2 + [VMEM if renew else ANY] * 2 + [HBM] * 6,
        out_specs=[VMEM] * 4 + [HBM] * 2,
        scratch_shapes=(
            pltpu.VMEM((3, 2, rows, cols), f32),
            pltpu.VMEM((count, side, side), f32),
            pltpu.VMEM((2, side, side), f32),
            pltpu.VMEM((side, 2 * side), bf16),
            pltpu.VMEM((2 * side, 2 * side), bf16),
            pltpu.VMEM((2 * side, 2 * side), bf16),
            pltpu.VMEM((3, 2, rows, cols), f32),
            pltpu.VMEM((2, side, side), f32),
            pltpu.VMEM((2, side, side), f32),
            pltpu.VMEM((2, side, side), f32),
            pltpu.VMEM((side, 2 * side), f32),
            pltpu.VMEM((2 * side, side), bf16),
            pltpu.SemaphoreType.DMA((8,)),
        ),
        compiler_params=pltpu.CompilerParams(vmem_limit_bytes=VMEM_LIMIT),
        input_output_aliases={5: 0, 2: 1, 3: 2, 4: 4, 6: 5} if renew else {},
        cost_estimate=pl.CostEstimate(
            flops=count * 64 * side**3, bytes_accessed=0, transcendentals=0
        ),
        name="update",
    )(ids, starts, own, other, *parts, amplitude, probe, table)


def hold(value, after):
    return pl.pallas_call(
        lambda *refs: None,
        out_shape=jax.ShapeDtypeStruct(value.shape, value.dtype),
        in_specs=[ANY, ANY],
        out_specs=ANY,
        input_output_aliases={0: 0},
        name="hold",
    )(value, after)


def relay(value, after):
    def kernel(value, out):
        out[...] = value[...]

    return call(kernel, shape(*value.shape), (value,), "relay", scalars=0, after=after)


def finish(ids, probe, own, other):
    def kernel(ids, probe, own, other, out):
        renewed(probe, own, other, ids[0], out)

    return call(kernel, shape(*probe.shape), (ids, probe, own, other), "finish")


def sum_and_repeat(value, copies, after):
    def kernel(value, out):
        added = value[0]
        for i in range(1, value.shape[0]):
            added = added + value[i]
        for i in range(copies):
            out[i] = added

    return call(kernel, shape(copies, *value.shape[1:]), (value,), "sum_repeat", scalars=0, after=after)


def add_into_ways(a, b, ways):
    return (a + b).reshape(ways, -1, a.shape[-1])


def spread_over(keep, give):
    plane = math.prod(lax.axis_size(a) for a in PLANE)
    return add_into_ways(keep, pair_swap(give, "core", 0), plane)


def widen(ids, tile, after=()):
    channels, rows, cols = tile.shape
    side = cols
    tags = rows - side

    def kernel(ids, near, tile, far, out):
        flip = ids[1]
        for ref, place in ((near, 2 * (1 - flip)), (tile, 1), (far, 2 * flip)):
            out[:, pl.ds(pl.multiple_of(side * place, side), side), :] = ref[:, :side, :]
            if tags:
                there = pl.ds(pl.multiple_of(3 * side + tags * place, tags), tags)
                out[:, there, :] = ref[:, side:, :]

    far = pair_swap(tile, ROW, 1)
    near = pair_swap(tile, ROW, 0)
    tall = call(kernel, shape(channels, 3 * rows, cols), (ids, near, tile, far), "stack", after=after)
    return pair_swap(tall, COL, 0), tall, pair_swap(tall, COL, 1)


def light(ids, spots, probe):
    side = probe.shape[-1]
    half = side // 2

    def kernel(ids, spots, probe, out, pad):
        core = ids[0]
        bright = probe[0] * probe[0] + probe[1] * probe[1]
        pad[...] = jnp.zeros_like(pad)
        pad[1, half : half + side, :] = bright[:, :half]
        pad[2, half : half + side, :] = bright[:, half:]
        added = jnp.zeros((half, half), f32)
        for k, beside in enumerate((1 - 2 * core, 0, 2 * core - 1)):
            for r in range(3):
                for p in range(spots.shape[2] // 2):
                    tag = spots[k, r, 2 * p]
                    u = jnp.where(tag > 0, side + 1 - tag - (r - 1) * half, 0)
                    v = side + 1 - spots[k, r, 2 * p + 1] - beside * half
                    v = jnp.where(tag > 0, v, 0)
                    lane = jnp.bitwise_and(v, half - 1)
                    block = lax.div(v, half)
                    here = pl.ds(u, half)
                    wide = jnp.concatenate([pad[block, here, :], pad[block + 1, here, :]], axis=1)
                    moved = pltpu.roll(wide, jnp.bitwise_and(side - lane, side - 1), 1)
                    added = added + moved[:, :half]
        out[...] = added

    return call(
        kernel,
        shape(half, half),
        (ids, spots, probe),
        "light",
        scratch=(pltpu.VMEM((5, 2 * side, half), f32),),
        scalars=2,
        flops=2 * 10**9,
    )


def split(ids, sib, mid, cross, after):
    channels, tall, cols = mid.shape
    rows = tall // 3

    def kernel(ids, mid, sib, cross, near, own, far):
        flip = ids[1]

        def part(start):
            here = pl.ds(start, rows)
            return mid[:, here, :] + sib[:, here, :] + cross[:, here, :]

        near[...] = part(pl.multiple_of(2 * rows * (1 - flip), rows))
        own[...] = part(rows)
        far[...] = part(pl.multiple_of(2 * rows * flip, rows))

    cross = pair_swap(cross, COL, 1)
    sib = pair_swap(sib, COL, 0)
    parts = [shape(channels, rows, cols)] * 3
    near, own, far = call(kernel, parts, (ids, mid, sib, cross), "split", after=after)
    return pair_swap(near, ROW, 0), own, pair_swap(far, ROW, 1)


def renew(tile, bright, near, own, far, after):
    def kernel(tile, bright, near, own, far, out):
        part = near[...] + own[...] + far[...]
        out[...] = tile[...] + part / (bright[...] + 1.0)

    operands = (tile, bright, near, own, far)
    return call(kernel, shape(*tile.shape), operands, "renew", scalars=0, after=after)


def on_device(patterns, background, offsets, probe, tile):
    side = probe.shape[-1]
    rows, cols = patterns.shape[:2]
    steps = jnp.stack(jnp.meshgrid(jnp.arange(rows), jnp.arange(cols), indexing="ij"), axis=-1)
    starts = (offsets + steps.astype(jnp.int32) * STEP).reshape(rows * cols, 2)
    ids = jnp.stack([lax.axis_index("core"), lax.axis_index("yl")]).astype(jnp.int32)
    amplitude = jnp.sqrt(jnp.maximum(patterns.reshape(rows * cols, side, side) - background, 0.0))
    table = jnp.asarray(dft_table(side))
    own = other = background
    tags = starts.reshape(1, 1, 2 * rows * cols).astype(f32) + 1.0
    tags = jnp.pad(tags, ((0, 0), (0, 7), (0, tile.shape[2] - tags.shape[2])))
    tags = jnp.broadcast_to(tags, (2,) + tags.shape[1:])
    parts = widen(ids, jnp.concatenate([tile, tags], axis=1))
    tall = side + side // 2
    spots = jnp.stack([v[0, tall::8, : 2 * rows * cols] for v in parts]).astype(jnp.int32)
    for step in range(ITERS):
        mid, keep, give, new_probe, sib, cross = update(
            step > 0, ids, starts, parts, amplitude, probe, own, other, table
        )
        if step > 0:
            probe = new_probe
        bright = light(ids, spots, probe)
        last = step == ITERS - 1
        part = spread_over(keep, give)
        ways, deep = part.shape[0], lax.axis_size("z")
        if last:
            cross = hold(cross, part)
        near, centre, far = split(ids, sib, mid, cross, (bright,))
        part = lax.all_to_all(part, PLANE, 0, 0)
        part = sum_and_repeat(part, deep, () if last else (centre,))
        if not last:
            tile = renew(tile, bright, near, centre, far, (part,))
        part = lax.all_to_all(part, "z", 0, 0)
        part = sum_and_repeat(part, ways, (centre,) if last else (tile,))
        if last:
            tile = renew(tile, bright, near, centre, far, ())
        else:
            parts = widen(ids, tile, (part,))
        own = lax.all_to_all(part, PLANE, 0, 0).reshape(side, side)
        if last:
            own = relay(own, (tile,))
        other = pair_swap(own, "core", 0)
    return tile, finish(ids, probe, own, other)


def solution(mesh):
    fine = Mesh(mesh.devices.reshape(4, 2, 8, 2, 2), ROW + COL)
    return jax.shard_map(
        on_device,
        mesh=fine,
        in_specs=(P(ROW, COL, None, None), P(), P(ROW, COL, None), P(), P(None, ROW, COL)),
        out_specs=(P(None, ROW, COL), P()),
        check_vma=False,
    )
```

```python
import math

import jax
import jax.numpy as jnp
import numpy as np
from jax import lax
from jax.experimental import pallas as pl
from jax.experimental.pallas import tpu as pltpu
from jax.sharding import Mesh, PartitionSpec as P

STEP = 64
ITERS = 2
ROW = ("x", "yl")
COL = ("z", "yh", "core")
PLANE = ("x", "yl", "yh")
CHUNK = 256
UNROLL = 1
VMEM_LIMIT = 14 * 1024 * 1024
SMALL = 8 * 1024 * 1024
f32 = jnp.float32
bf16 = jnp.bfloat16
VMEM = pl.BlockSpec(memory_space=pltpu.VMEM)
HBM = pl.BlockSpec(memory_space=pltpu.HBM)
ANY = pl.BlockSpec(memory_space=pl.ANY)
SMEM = pl.BlockSpec(memory_space=pltpu.SMEM)


def dft_table(side_len):
    index = np.arange(side_len)
    angles = (np.outer(index, index) % side_len).astype(np.float32) * np.float32(
        2.0 * math.pi / side_len
    )
    scaling = np.float32(1.0 / math.sqrt(side_len))
    real = np.cos(angles) * scaling
    imag = -np.sin(angles) * scaling
    return np.concatenate([real, imag], axis=1).astype(bf16)


def call(kernel, out_shape, operands, name, scratch=(), scalars=1, flops=0, limit=SMALL, after=()):
    many = isinstance(out_shape, (tuple, list))
    moved = sum(math.prod(o.shape) * o.dtype.itemsize for o in operands)
    waits = len(after)

    def body(*refs):
        kernel(*refs[waits:])

    operands = (*after, *operands)
    return pl.pallas_call(
        body,
        out_shape=out_shape,
        in_specs=[ANY] * waits
        + [SMEM] * scalars
        + [VMEM] * (len(operands) - scalars - waits),
        out_specs=[VMEM] * len(out_shape) if many else VMEM,
        scratch_shapes=list(scratch),
        compiler_params=pltpu.CompilerParams(vmem_limit_bytes=limit),
        cost_estimate=pl.CostEstimate(flops=flops, bytes_accessed=moved, transcendentals=0),
        name=name,
    )(*operands)


def shape(*dims):
    return jax.ShapeDtypeStruct(dims, f32)


def pair_swap(value, axis, first):
    count = lax.axis_size(axis)
    pairs = []
    for i in range(first, count - 1, 2):
        pairs += [(i, i + 1), (i + 1, i)]
    return lax.ppermute(value, axis, pairs)


def renewed(probe, own, other, core, out):
    side = probe.shape[-1]
    square = jnp.zeros((8, side), f32)
    for part in (own, other):
        part = part[...]
        square = square + jnp.sum((part * part).reshape(side // 8, 8, side), axis=0)
    spread = jnp.sqrt(jnp.sum(square) / (2.0 * side * side) + 1e-06)
    scale = jnp.full((8, side), 1.0, f32) / spread
    scale = jnp.broadcast_to(scale[None], (side // 8, 8, side)).reshape(side, side)
    out[core] = probe[core] + own[...] * scale
    out[1 - core] = probe[1 - core] + other[...] * scale


def update_kernel(renew, ids, starts, own, other, sib, mid, cross, amplitude_in, probe_in, table_in,
                  mid_out, keep, give, probe_out, sib_out, cross_out,
                  strips, amplitude, probe, table, first, second, acc, grad, window, wave, field, bent, sems):
    side = probe.shape[-1]
    count = amplitude.shape[0]
    chunks = side // CHUNK
    core = ids[0]
    near, far = 2 * (1 - core), 2 * core
    tall = pl.ds(0, side + side // 2)
    moves = [
        pltpu.make_async_copy(a, b, sems.at[n])
        for n, (a, b) in enumerate((
            (probe_in, probe),
            (mid.at[:, tall], strips.at[1]),
            (sib.at[:, tall], strips.at[near]),
            (cross.at[:, tall], strips.at[far]),
            (table_in, table),
            (amplitude_in, amplitude),
            (acc.at[near], sib_out),
            (acc.at[far], cross_out),
        ))
    ]
    for move in moves[:6]:
        move.start()
    acc[...] = jnp.zeros_like(acc)
    moves[0].wait()
    if renew:
        renewed(probe, own, other, core, probe)
        probe_out[...] = probe[...]
    else:
        probe_out[...] = jnp.zeros_like(probe_out)
    for move in moves[1:4]:
        move.wait()
    for p in range(count):
        row_start = starts[p, 0]
        col_start = starts[p, 1]

        def load(i, _):
            here = pl.ds(pl.multiple_of(i * CHUNK, CHUNK), CHUNK)
            there = pl.ds(row_start + i * CHUNK, CHUNK)
            cut = []
            for c in range(2):
                wide = jnp.concatenate([strips[k, c, there, :] for k in range(3)], axis=1)
                part = pltpu.roll(wide, 3 * 128 - col_start, 1)[:, :side]
                window[c, here, :] = part
                cut.append(part)
            pr, pi = probe[0, here, :], probe[1, here, :]
            er = pr * cut[0] - pi * cut[1]
            ei = pr * cut[1] + pi * cut[0]
            wave[0, here, :] = er
            wave[1, here, :] = ei
            bent[here, :] = er.astype(bf16)
            bent[pl.ds(pl.multiple_of(side + i * CHUNK, CHUNK), CHUNK), :] = ei.astype(bf16)
            return 0

        lax.fori_loop(0, chunks, load, 0, unroll=UNROLL)
        if p == 0:
            for move in moves[4:6]:
                move.wait()
            real, imag = table[:, :side], table[:, side:]
            first[:side, :side] = real
            first[:side, side:] = -imag
            first[side:, :side] = imag
            first[side:, side:] = real
            second[:side, :side] = real
            second[:side, side:] = imag
            second[side:, :side] = -imag
            second[side:, side:] = real
        half = jnp.dot(first[...], bent[...], preferred_element_type=f32).astype(bf16)
        half = jnp.concatenate([half[:side], half[side:]], axis=1)
        field[...] = jnp.dot(half, second[...], preferred_element_type=f32)

        def project(i, _):
            here = pl.ds(pl.multiple_of(i * CHUNK, CHUNK), CHUNK)
            fr, fi = field[here, :side], field[here, side:]
            scale = amplitude[p, here, :] * lax.rsqrt(jnp.maximum(fr * fr + fi * fi, 0.25))
            bent[here, :] = (fr * scale).astype(bf16)
            bent[pl.ds(pl.multiple_of(side + i * CHUNK, CHUNK), CHUNK), :] = (fi * scale).astype(bf16)
            return 0

        lax.fori_loop(0, chunks, project, 0, unroll=UNROLL)
        half = jnp.dot(second[...], bent[...], preferred_element_type=f32).astype(bf16)
        half = jnp.concatenate([half[:side], half[side:]], axis=1)
        field[...] = jnp.dot(half, first[...], preferred_element_type=f32)

        def spread_out(i, _):
            here = pl.ds(pl.multiple_of(i * CHUNK, CHUNK), CHUNK)
            there = pl.ds(row_start + i * CHUNK, CHUNK)
            dr = field[here, :side] - wave[0, here, :]
            di = field[here, side:] - wave[1, here, :]
            pr, pi = probe[0, here, :], probe[1, here, :]
            wr, wi = window[0, here, :], window[1, here, :]
            gr = wr * dr + wi * di
            gi = wr * di - wi * dr
            if p > 0:
                gr = gr + grad[0, here, :]
                gi = gi + grad[1, here, :]
            if p < count - 1:
                grad[0, here, :] = gr
                grad[1, here, :] = gi
            else:
                keep[here, :] = jnp.where(core == 0, gr, gi)
                give[here, :] = jnp.where(core == 0, gi, gr)
            terms = (pr * dr + pi * di, pr * di - pi * dr)
            for c, term in enumerate(terms):
                wide = jnp.concatenate([term, jnp.zeros((CHUNK, 128), f32)], axis=1)
                moved = pltpu.roll(wide, col_start, 1)
                for k in range(3):
                    acc[k, c, there, :] += moved[:, 128 * k : 128 * (k + 1)]
            return 0

        lax.fori_loop(0, chunks, spread_out, 0, unroll=UNROLL)
    moves[6].start()
    moves[7].start()
    mid_out[...] = acc[1]
    for move in moves[6:]:
        move.wait()


def update(renew, ids, starts, parts, amplitude, probe, own, other, table):
    side = probe.shape[-1]
    rows, cols = side + side // 2, parts[0].shape[2]
    strip, square, wave = shape(2, rows, cols), shape(side, side), shape(2, side, side)
    count = amplitude.shape[0]
    if not renew:
        wave = shape(8, 128)
    return pl.pallas_call(
        lambda *refs: update_kernel(renew, *refs),
        out_shape=(strip, square, square, wave, strip, strip),
        in_specs=[SMEM] * 2 + [VMEM if renew else ANY] * 2 + [HBM] * 6,
        out_specs=[VMEM] * 4 + [HBM] * 2,
        scratch_shapes=(
            pltpu.VMEM((3, 2, rows, cols), f32),
            pltpu.VMEM((count, side, side), f32),
            pltpu.VMEM((2, side, side), f32),
            pltpu.VMEM((side, 2 * side), bf16),
            pltpu.VMEM((2 * side, 2 * side), bf16),
            pltpu.VMEM((2 * side, 2 * side), bf16),
            pltpu.VMEM((3, 2, rows, cols), f32),
            pltpu.VMEM((2, side, side), f32),
            pltpu.VMEM((2, side, side), f32),
            pltpu.VMEM((2, side, side), f32),
            pltpu.VMEM((side, 2 * side), f32),
            pltpu.VMEM((2 * side, side), bf16),
            pltpu.SemaphoreType.DMA((8,)),
        ),
        compiler_params=pltpu.CompilerParams(vmem_limit_bytes=VMEM_LIMIT),
        input_output_aliases={5: 0, 2: 1, 3: 2, 4: 4, 6: 5} if renew else {},
        cost_estimate=pl.CostEstimate(
            flops=count * 64 * side**3, bytes_accessed=0, transcendentals=0
        ),
        name="update",
    )(ids, starts, own, other, *parts, amplitude, probe, table)


def hold(value, after):
    return pl.pallas_call(
        lambda *refs: None,
        out_shape=jax.ShapeDtypeStruct(value.shape, value.dtype),
        in_specs=[ANY, ANY],
        out_specs=ANY,
        input_output_aliases={0: 0},
        name="hold",
    )(value, after)


def relay(value, after):
    def kernel(value, out):
        out[...] = value[...]

    return call(kernel, shape(*value.shape), (value,), "relay", scalars=0, after=after)


def finish(ids, probe, own, other):
    def kernel(ids, probe, own, other, out):
        renewed(probe, own, other, ids[0], out)

    return call(kernel, shape(*probe.shape), (ids, probe, own, other), "finish")


def sum_and_repeat(value, copies, after):
    def kernel(value, out):
        added = value[0]
        for i in range(1, value.shape[0]):
            added = added + value[i]
        for i in range(copies):
            out[i] = added

    return call(kernel, shape(copies, *value.shape[1:]), (value,), "sum_repeat", scalars=0, after=after)


def add_into_ways(a, b, ways):
    def kernel(a, b, out):
        out[...] = a[...] + b[...]

    return call(kernel, shape(*a.shape), (a, b), "add", scalars=0).reshape(ways, -1, a.shape[-1])


def spread_over(keep, give):
    plane = math.prod(lax.axis_size(a) for a in PLANE)
    return add_into_ways(keep, pair_swap(give, "core", 0), plane)


def widen(ids, tile, after=()):
    channels, rows, cols = tile.shape
    side = cols
    tags = rows - side

    def kernel(ids, near, tile, far, out):
        flip = ids[1]
        for ref, place in ((near, 2 * (1 - flip)), (tile, 1), (far, 2 * flip)):
            out[:, pl.ds(pl.multiple_of(side * place, side), side), :] = ref[:, :side, :]
            if tags:
                there = pl.ds(pl.multiple_of(3 * side + tags * place, tags), tags)
                out[:, there, :] = ref[:, side:, :]

    far = pair_swap(tile, ROW, 1)
    near = pair_swap(tile, ROW, 0)
    tall = call(kernel, shape(channels, 3 * rows, cols), (ids, near, tile, far), "stack", after=after)
    return pair_swap(tall, COL, 0), tall, pair_swap(tall, COL, 1)


def light(ids, spots, probe):
    side = probe.shape[-1]
    half = side // 2

    def kernel(ids, spots, probe, out, pad):
        core = ids[0]
        bright = probe[0] * probe[0] + probe[1] * probe[1]
        pad[...] = jnp.zeros_like(pad)
        pad[1, half : half + side, :] = bright[:, :half]
        pad[2, half : half + side, :] = bright[:, half:]
        added = jnp.zeros((half, half), f32)
        for k, beside in enumerate((1 - 2 * core, 0, 2 * core - 1)):
            for r in range(3):
                for p in range(spots.shape[2] // 2):
                    tag = spots[k, r, 2 * p]
                    u = jnp.where(tag > 0, side + 1 - tag - (r - 1) * half, 0)
                    v = side + 1 - spots[k, r, 2 * p + 1] - beside * half
                    v = jnp.where(tag > 0, v, 0)
                    lane = jnp.bitwise_and(v, half - 1)
                    block = lax.div(v, half)
                    here = pl.ds(u, half)
                    wide = jnp.concatenate([pad[block, here, :], pad[block + 1, here, :]], axis=1)
                    moved = pltpu.roll(wide, jnp.bitwise_and(side - lane, side - 1), 1)
                    added = added + moved[:, :half]
        out[...] = added

    return call(
        kernel,
        shape(half, half),
        (ids, spots, probe),
        "light",
        scratch=(pltpu.VMEM((5, 2 * side, half), f32),),
        scalars=2,
        flops=2 * 10**9,
    )


def split(ids, sib, mid, cross, after):
    channels, tall, cols = mid.shape
    rows = tall // 3

    def kernel(ids, mid, sib, cross, near, own, far):
        flip = ids[1]

        def part(start):
            here = pl.ds(start, rows)
            return mid[:, here, :] + sib[:, here, :] + cross[:, here, :]

        near[...] = part(pl.multiple_of(2 * rows * (1 - flip), rows))
        own[...] = part(rows)
        far[...] = part(pl.multiple_of(2 * rows * flip, rows))

    cross = pair_swap(cross, COL, 1)
    sib = pair_swap(sib, COL, 0)
    parts = [shape(channels, rows, cols)] * 3
    near, own, far = call(kernel, parts, (ids, mid, sib, cross), "split", after=after)
    return pair_swap(near, ROW, 0), own, pair_swap(far, ROW, 1)


def renew(tile, bright, near, own, far, after):
    def kernel(tile, bright, near, own, far, out):
        part = near[...] + own[...] + far[...]
        out[...] = tile[...] + part / (bright[...] + 1.0)

    operands = (tile, bright, near, own, far)
    return call(kernel, shape(*tile.shape), operands, "renew", scalars=0, after=after)


def on_device(patterns, background, offsets, probe, tile):
    side = probe.shape[-1]
    rows, cols = patterns.shape[:2]
    steps = jnp.stack(jnp.meshgrid(jnp.arange(rows), jnp.arange(cols), indexing="ij"), axis=-1)
    starts = (offsets + steps.astype(jnp.int32) * STEP).reshape(rows * cols, 2)
    ids = jnp.stack([lax.axis_index("core"), lax.axis_index("yl")]).astype(jnp.int32)
    amplitude = jnp.sqrt(jnp.maximum(patterns.reshape(rows * cols, side, side) - background, 0.0))
    table = jnp.asarray(dft_table(side))
    own = other = background
    tags = starts.reshape(1, 1, 2 * rows * cols).astype(f32) + 1.0
    tags = jnp.pad(tags, ((0, 0), (0, 7), (0, tile.shape[2] - tags.shape[2])))
    tags = jnp.broadcast_to(tags, (2,) + tags.shape[1:])
    parts = widen(ids, jnp.concatenate([tile, tags], axis=1))
    for step in range(ITERS):
        mid, keep, give, new_probe, sib, cross = update(
            step > 0, ids, starts, parts, amplitude, probe, own, other, table
        )
        if step > 0:
            probe = new_probe
        last = step == ITERS - 1
        part = spread_over(keep, give)
        ways, deep = part.shape[0], lax.axis_size("z")
        if last:
            cross = hold(cross, part)
        else:
            tall, width = side + side // 2, 2 * rows * cols
            spots = (parts[0], parts[1], hold(parts[2], part))
            spots = jnp.stack([v[0, tall::8, :width] for v in spots]).astype(jnp.int32)
        bright = light(ids, spots, probe)
        near, centre, far = split(ids, sib, mid, cross, (bright,))
        part = lax.all_to_all(part, PLANE, 0, 0)
        part = sum_and_repeat(part, deep, () if last else (centre,))
        if not last:
            tile = renew(tile, bright, near, centre, far, (part,))
        part = lax.all_to_all(part, "z", 0, 0)
        part = sum_and_repeat(part, ways, (centre,) if last else (tile,))
        if last:
            tile = renew(tile, bright, near, centre, far, ())
        else:
            parts = widen(ids, tile, (part,))
        own = lax.all_to_all(part, PLANE, 0, 0).reshape(side, side)
        if last:
            own = relay(own, (tile,))
        other = pair_swap(own, "core", 0)
    return tile, finish(ids, probe, own, other)


def solution(mesh):
    fine = Mesh(mesh.devices.reshape(4, 2, 8, 2, 2), ROW + COL)
    return jax.shard_map(
        on_device,
        mesh=fine,
        in_specs=(P(ROW, COL, None, None), P(), P(ROW, COL, None), P(), P(None, ROW, COL)),
        out_specs=(P(None, ROW, COL), P()),
        check_vma=False,
    )
```

```python
import math

import jax
import jax.numpy as jnp
import numpy as np
from jax import lax
from jax.experimental import pallas as pl
from jax.experimental.pallas import tpu as pltpu
from jax.sharding import Mesh, PartitionSpec as P

STEP = 64
ITERS = 2
ROW = ("x", "yl")
COL = ("z", "yh", "core")
PLANE = ("x", "yl", "yh")
CHUNK = 256
UNROLL = 1
VMEM_LIMIT = 14 * 1024 * 1024
SMALL = 8 * 1024 * 1024
f32 = jnp.float32
bf16 = jnp.bfloat16
VMEM = pl.BlockSpec(memory_space=pltpu.VMEM)
HBM = pl.BlockSpec(memory_space=pltpu.HBM)
ANY = pl.BlockSpec(memory_space=pl.ANY)
SMEM = pl.BlockSpec(memory_space=pltpu.SMEM)


def dft_table(side_len):
    index = np.arange(side_len)
    angles = (np.outer(index, index) % side_len).astype(np.float32) * np.float32(
        2.0 * math.pi / side_len
    )
    scaling = np.float32(1.0 / math.sqrt(side_len))
    real = np.cos(angles) * scaling
    imag = -np.sin(angles) * scaling
    return np.concatenate([real, imag], axis=1).astype(bf16)


def call(kernel, out_shape, operands, name, scratch=(), scalars=1, flops=0, limit=SMALL, after=()):
    many = isinstance(out_shape, (tuple, list))
    moved = sum(math.prod(o.shape) * o.dtype.itemsize for o in operands)
    waits = len(after)

    def body(*refs):
        kernel(*refs[waits:])

    operands = (*after, *operands)
    return pl.pallas_call(
        body,
        out_shape=out_shape,
        in_specs=[ANY] * waits
        + [SMEM] * scalars
        + [VMEM] * (len(operands) - scalars - waits),
        out_specs=[VMEM] * len(out_shape) if many else VMEM,
        scratch_shapes=list(scratch),
        compiler_params=pltpu.CompilerParams(vmem_limit_bytes=limit),
        cost_estimate=pl.CostEstimate(flops=flops, bytes_accessed=moved, transcendentals=0),
        name=name,
    )(*operands)


def shape(*dims):
    return jax.ShapeDtypeStruct(dims, f32)


def pair_swap(value, axis, first):
    count = lax.axis_size(axis)
    pairs = []
    for i in range(first, count - 1, 2):
        pairs += [(i, i + 1), (i + 1, i)]
    return lax.ppermute(value, axis, pairs)


def renewed(probe, own, other, core, out):
    side = probe.shape[-1]
    square = jnp.zeros((8, side), f32)
    for part in (own, other):
        part = part[...]
        square = square + jnp.sum((part * part).reshape(side // 8, 8, side), axis=0)
    spread = jnp.sqrt(jnp.sum(square) / (2.0 * side * side) + 1e-06)
    scale = jnp.full((8, side), 1.0, f32) / spread
    scale = jnp.broadcast_to(scale[None], (side // 8, 8, side)).reshape(side, side)
    out[core] = probe[core] + own[...] * scale
    out[1 - core] = probe[1 - core] + other[...] * scale


def update_kernel(renew, ids, starts, own, other, sib, mid, cross, amplitude_in, probe_in, table_in,
                  mid_out, keep, give, probe_out, sib_out, cross_out,
                  strips, amplitude, probe, table, first, second, acc, grad, window, wave, field, bent, sems):
    side = probe.shape[-1]
    count = amplitude.shape[0]
    chunks = side // CHUNK
    core = ids[0]
    near, far = 2 * (1 - core), 2 * core
    tall = pl.ds(0, side + side // 2)
    moves = [
        pltpu.make_async_copy(a, b, sems.at[n])
        for n, (a, b) in enumerate((
            (probe_in, probe),
            (mid.at[:, tall], strips.at[1]),
            (sib.at[:, tall], strips.at[near]),
            (cross.at[:, tall], strips.at[far]),
            (table_in, table),
            (amplitude_in, amplitude),
            (acc.at[near], sib_out),
            (acc.at[far], cross_out),
        ))
    ]
    for move in moves[:6]:
        move.start()
    acc[...] = jnp.zeros_like(acc)
    moves[0].wait()
    if renew:
        renewed(probe, own, other, core, probe)
        probe_out[...] = probe[...]
    else:
        probe_out[...] = jnp.zeros_like(probe_out)
    for move in moves[1:4]:
        move.wait()
    for p in range(count):
        row_start = starts[p, 0]
        col_start = starts[p, 1]

        def load(i, _):
            here = pl.ds(pl.multiple_of(i * CHUNK, CHUNK), CHUNK)
            there = pl.ds(row_start + i * CHUNK, CHUNK)
            cut = []
            for c in range(2):
                wide = jnp.concatenate([strips[k, c, there, :] for k in range(3)], axis=1)
                part = pltpu.roll(wide, 3 * 128 - col_start, 1)[:, :side]
                window[c, here, :] = part
                cut.append(part)
            pr, pi = probe[0, here, :], probe[1, here, :]
            er = pr * cut[0] - pi * cut[1]
            ei = pr * cut[1] + pi * cut[0]
            wave[0, here, :] = er
            wave[1, here, :] = ei
            bent[here, :] = er.astype(bf16)
            bent[pl.ds(pl.multiple_of(side + i * CHUNK, CHUNK), CHUNK), :] = ei.astype(bf16)
            return 0

        lax.fori_loop(0, chunks, load, 0, unroll=UNROLL)
        if p == 0:
            for move in moves[4:6]:
                move.wait()
            real, imag = table[:, :side], table[:, side:]
            first[:side, :side] = real
            first[:side, side:] = -imag
            first[side:, :side] = imag
            first[side:, side:] = real
            second[:side, :side] = real
            second[:side, side:] = imag
            second[side:, :side] = -imag
            second[side:, side:] = real
        half = jnp.dot(first[...], bent[...], preferred_element_type=f32).astype(bf16)
        half = jnp.concatenate([half[:side], half[side:]], axis=1)
        field[...] = jnp.dot(half, second[...], preferred_element_type=f32)

        def project(i, _):
            here = pl.ds(pl.multiple_of(i * CHUNK, CHUNK), CHUNK)
            fr, fi = field[here, :side], field[here, side:]
            scale = amplitude[p, here, :] * lax.rsqrt(jnp.maximum(fr * fr + fi * fi, 0.25))
            bent[here, :] = (fr * scale).astype(bf16)
            bent[pl.ds(pl.multiple_of(side + i * CHUNK, CHUNK), CHUNK), :] = (fi * scale).astype(bf16)
            return 0

        lax.fori_loop(0, chunks, project, 0, unroll=UNROLL)
        half = jnp.dot(second[...], bent[...], preferred_element_type=f32).astype(bf16)
        half = jnp.concatenate([half[:side], half[side:]], axis=1)
        field[...] = jnp.dot(half, first[...], preferred_element_type=f32)

        def spread_out(i, _):
            here = pl.ds(pl.multiple_of(i * CHUNK, CHUNK), CHUNK)
            there = pl.ds(row_start + i * CHUNK, CHUNK)
            dr = field[here, :side] - wave[0, here, :]
            di = field[here, side:] - wave[1, here, :]
            pr, pi = probe[0, here, :], probe[1, here, :]
            wr, wi = window[0, here, :], window[1, here, :]
            gr = wr * dr + wi * di
            gi = wr * di - wi * dr
            if p > 0:
                gr = gr + grad[0, here, :]
                gi = gi + grad[1, here, :]
            if p < count - 1:
                grad[0, here, :] = gr
                grad[1, here, :] = gi
            else:
                keep[here, :] = jnp.where(core == 0, gr, gi)
                give[here, :] = jnp.where(core == 0, gi, gr)
            terms = (pr * dr + pi * di, pr * di - pi * dr)
            for c, term in enumerate(terms):
                wide = jnp.concatenate([term, jnp.zeros((CHUNK, 128), f32)], axis=1)
                moved = pltpu.roll(wide, col_start, 1)
                for k in range(3):
                    acc[k, c, there, :] += moved[:, 128 * k : 128 * (k + 1)]
            return 0

        lax.fori_loop(0, chunks, spread_out, 0, unroll=UNROLL)
    moves[6].start()
    moves[7].start()
    mid_out[...] = acc[1]
    for move in moves[6:]:
        move.wait()


def update(renew, ids, starts, parts, amplitude, probe, own, other, table):
    side = probe.shape[-1]
    rows, cols = side + side // 2, parts[0].shape[2]
    strip, square, wave = shape(2, rows, cols), shape(side, side), shape(2, side, side)
    count = amplitude.shape[0]
    if not renew:
        wave = shape(8, 128)
    return pl.pallas_call(
        lambda *refs: update_kernel(renew, *refs),
        out_shape=(strip, square, square, wave, strip, strip),
        in_specs=[SMEM] * 2 + [VMEM if renew else ANY] * 2 + [HBM] * 6,
        out_specs=[VMEM] * 4 + [HBM] * 2,
        scratch_shapes=(
            pltpu.VMEM((3, 2, rows, cols), f32),
            pltpu.VMEM((count, side, side), f32),
            pltpu.VMEM((2, side, side), f32),
            pltpu.VMEM((side, 2 * side), bf16),
            pltpu.VMEM((2 * side, 2 * side), bf16),
            pltpu.VMEM((2 * side, 2 * side), bf16),
            pltpu.VMEM((3, 2, rows, cols), f32),
            pltpu.VMEM((2, side, side), f32),
            pltpu.VMEM((2, side, side), f32),
            pltpu.VMEM((2, side, side), f32),
            pltpu.VMEM((side, 2 * side), f32),
            pltpu.VMEM((2 * side, side), bf16),
            pltpu.SemaphoreType.DMA((8,)),
        ),
        compiler_params=pltpu.CompilerParams(vmem_limit_bytes=VMEM_LIMIT),
        input_output_aliases={5: 0, 2: 1, 3: 2, 4: 4, 6: 5} if renew else {},
        cost_estimate=pl.CostEstimate(
            flops=count * 64 * side**3, bytes_accessed=0, transcendentals=0
        ),
        name="update",
    )(ids, starts, own, other, *parts, amplitude, probe, table)


def hold(value, after):
    return pl.pallas_call(
        lambda *refs: None,
        out_shape=jax.ShapeDtypeStruct(value.shape, value.dtype),
        in_specs=[ANY, ANY],
        out_specs=ANY,
        input_output_aliases={0: 0},
        name="hold",
    )(value, after)


def relay(value, after):
    def kernel(value, out):
        out[...] = value[...]

    return call(kernel, shape(*value.shape), (value,), "relay", scalars=0, after=after)


def finish(ids, probe, own, other):
    def kernel(ids, probe, own, other, out):
        renewed(probe, own, other, ids[0], out)

    return call(kernel, shape(*probe.shape), (ids, probe, own, other), "finish")


def sum_and_repeat(value, copies, after):
    def kernel(value, out):
        added = value[0]
        for i in range(1, value.shape[0]):
            added = added + value[i]
        for i in range(copies):
            out[i] = added

    return call(kernel, shape(copies, *value.shape[1:]), (value,), "sum_repeat", scalars=0, after=after)


def add_into_ways(a, b, ways):
    def kernel(a, b, out):
        out[...] = a[...] + b[...]

    return call(kernel, shape(*a.shape), (a, b), "add", scalars=0).reshape(ways, -1, a.shape[-1])


def spread_over(keep, give):
    plane = math.prod(lax.axis_size(a) for a in PLANE)
    return add_into_ways(keep, pair_swap(give, "core", 0), plane)


def widen(ids, tile, after=()):
    channels, rows, cols = tile.shape
    side = cols
    tags = rows - side

    def kernel(ids, near, tile, far, out):
        flip = ids[1]
        for ref, place in ((near, 2 * (1 - flip)), (tile, 1), (far, 2 * flip)):
            out[:, pl.ds(pl.multiple_of(side * place, side), side), :] = ref[:, :side, :]
            if tags:
                there = pl.ds(pl.multiple_of(3 * side + tags * place, tags), tags)
                out[:, there, :] = ref[:, side:, :]

    far = pair_swap(tile, ROW, 1)
    near = pair_swap(tile, ROW, 0)
    tall = call(kernel, shape(channels, 3 * rows, cols), (ids, near, tile, far), "stack", after=after)
    return pair_swap(tall, COL, 0), tall, pair_swap(tall, COL, 1)


def light(ids, spots, probe):
    side = probe.shape[-1]
    half = side // 2

    def kernel(ids, spots, probe, out, pad):
        core = ids[0]
        bright = probe[0] * probe[0] + probe[1] * probe[1]
        pad[...] = jnp.zeros_like(pad)
        pad[1, half : half + side, :] = bright[:, :half]
        pad[2, half : half + side, :] = bright[:, half:]
        added = jnp.zeros((half, half), f32)
        for k, beside in enumerate((1 - 2 * core, 0, 2 * core - 1)):
            for r in range(3):
                for p in range(spots.shape[2] // 2):
                    tag = spots[k, r, 2 * p]
                    u = jnp.where(tag > 0, side + 1 - tag - (r - 1) * half, 0)
                    v = side + 1 - spots[k, r, 2 * p + 1] - beside * half
                    v = jnp.where(tag > 0, v, 0)
                    lane = jnp.bitwise_and(v, half - 1)
                    block = lax.div(v, half)
                    here = pl.ds(u, half)
                    wide = jnp.concatenate([pad[block, here, :], pad[block + 1, here, :]], axis=1)
                    moved = pltpu.roll(wide, jnp.bitwise_and(side - lane, side - 1), 1)
                    added = added + moved[:, :half]
        out[...] = added

    return call(
        kernel,
        shape(half, half),
        (ids, spots, probe),
        "light",
        scratch=(pltpu.VMEM((5, 2 * side, half), f32),),
        scalars=2,
        flops=2 * 10**9,
    )


def split(ids, sib, mid, cross, after):
    channels, tall, cols = mid.shape
    rows = tall // 3

    def kernel(ids, mid, sib, cross, near, own, far):
        flip = ids[1]

        def part(start):
            here = pl.ds(start, rows)
            return mid[:, here, :] + sib[:, here, :] + cross[:, here, :]

        near[...] = part(pl.multiple_of(2 * rows * (1 - flip), rows))
        own[...] = part(rows)
        far[...] = part(pl.multiple_of(2 * rows * flip, rows))

    cross = pair_swap(cross, COL, 1)
    sib = pair_swap(sib, COL, 0)
    parts = [shape(channels, rows, cols)] * 3
    near, own, far = call(kernel, parts, (ids, mid, sib, cross), "split", after=after)
    return pair_swap(near, ROW, 0), own, pair_swap(far, ROW, 1)


def renew(tile, bright, near, own, far, after):
    def kernel(tile, bright, near, own, far, out):
        part = near[...] + own[...] + far[...]
        out[...] = tile[...] + part / (bright[...] + 1.0)

    operands = (tile, bright, near, own, far)
    return call(kernel, shape(*tile.shape), operands, "renew", scalars=0, after=after)


def on_device(patterns, background, offsets, probe, tile):
    side = probe.shape[-1]
    rows, cols = patterns.shape[:2]
    steps = jnp.stack(jnp.meshgrid(jnp.arange(rows), jnp.arange(cols), indexing="ij"), axis=-1)
    starts = (offsets + steps.astype(jnp.int32) * STEP).reshape(rows * cols, 2)
    ids = jnp.stack([lax.axis_index("core"), lax.axis_index("yl")]).astype(jnp.int32)
    amplitude = jnp.sqrt(jnp.maximum(patterns.reshape(rows * cols, side, side) - background, 0.0))
    table = jnp.asarray(dft_table(side))
    own = other = background
    tags = starts.reshape(1, 1, 2 * rows * cols).astype(f32) + 1.0
    tags = jnp.pad(tags, ((0, 0), (0, 7), (0, tile.shape[2] - tags.shape[2])))
    tags = jnp.broadcast_to(tags, (2,) + tags.shape[1:])
    parts = widen(ids, jnp.concatenate([tile, tags], axis=1))
    for step in range(ITERS):
        mid, keep, give, new_probe, sib, cross = update(
            step > 0, ids, starts, parts, amplitude, probe, own, other, table
        )
        if step > 0:
            probe = new_probe
        last = step == ITERS - 1
        part = spread_over(keep, give)
        ways, deep = part.shape[0], lax.axis_size("z")
        if last:
            cross = hold(cross, part)
        else:
            tall, width = side + side // 2, 2 * rows * cols
            spots = (parts[0], parts[1], hold(parts[2], part))
            spots = jnp.stack([v[0, tall::8, :width] for v in spots]).astype(jnp.int32)
        bright = light(ids, spots, probe)
        near, centre, far = split(ids, sib, mid, cross, (bright,))
        part = lax.all_to_all(part, PLANE, 0, 0)
        part = sum_and_repeat(part, deep, () if last else (near,))
        if not last:
            tile = renew(tile, bright, near, centre, far, (part,))
        part = lax.all_to_all(part, "z", 0, 0)
        part = sum_and_repeat(part, ways, (near,) if last else (tile,))
        if last:
            tile = renew(tile, bright, near, centre, far, ())
        else:
            parts = widen(ids, tile, (part,))
        own = lax.all_to_all(part, PLANE, 0, 0).reshape(side, side)
        if last:
            own = relay(own, (tile,))
        other = pair_swap(own, "core", 0)
    return tile, finish(ids, probe, own, other)


def solution(mesh):
    fine = Mesh(mesh.devices.reshape(4, 2, 8, 2, 2), ROW + COL)
    return jax.shard_map(
        on_device,
        mesh=fine,
        in_specs=(P(ROW, COL, None, None), P(), P(ROW, COL, None), P(), P(None, ROW, COL)),
        out_specs=(P(None, ROW, COL), P()),
        check_vma=False,
    )
```
